256 devices in a mesh: expert: 64 (over y, z, core), dp: 4 (over x).
Axes of the slice: x: 4, y: 4, z: 8, core: 2. Of those that a mesh axis runs over, the one named last changes fastest.
Arguments:
- tokens: bfloat16 [32768, 2048], P(('expert', 'dp')), may hold values from -24 to 24
- cotangent: bfloat16 [32768, 2048], P(('expert', 'dp')), may hold values from -3 to 3
- route_ids: int32 [32768, 2], P(('expert', 'dp')), may hold values from 0 to 64, as said below
- route_weights: float32 [32768, 2], P(('expert', 'dp')), may hold values from 0.2 to 1
- cold_gate: bfloat16 [64, 768, 2048], P('expert', 'dp'), may hold values from -0.125 to 0.125
- cold_up: bfloat16 [64, 768, 2048], P('expert', 'dp'), may hold values from -0.125 to 0.125
- cold_down: bfloat16 [64, 768, 2048], P('expert', 'dp'), may hold values from -0.21875 to 0.21875
- hot_gate: bfloat16 [1, 768, 2048], P(None, 'dp'), may hold values from -0.125 to 0.125
- hot_up: bfloat16 [1, 768, 2048], P(None, 'dp'), may hold values from -0.125 to 0.125
- hot_down: bfloat16 [1, 768, 2048], P(None, 'dp'), may hold values from -0.21875 to 0.21875
Outputs:
- mixed: bfloat16 [32768, 2048], P(('expert', 'dp'))
- token_grad: bfloat16 [32768, 2048], P(('expert', 'dp'))
- route_grad: float32 [32768, 2], P(('expert', 'dp'))
- cold_gate_grad: bfloat16 [64, 768, 2048], P('expert', 'dp')
- cold_up_grad: bfloat16 [64, 768, 2048], P('expert', 'dp')
- cold_down_grad: bfloat16 [64, 768, 2048], P('expert', 'dp')
- hot_gate_grad: float32 [1, 768, 2048], P(None, 'dp', 'expert')
- hot_up_grad: float32 [1, 768, 2048], P(None, 'dp', 'expert')
- hot_down_grad: float32 [1, 768, 2048], P(None, 'dp', 'expert')
The draws below stay inside these ranges and needn't reach their ends.
Inputs may be any that keep to these rules, and one draw needn't show every extreme that they name: `route_ids`: each row names 2 different experts. Experts 64 and above are the hot ones; among the rows of one device each hot expert is named exactly 32 times, no row names two hot experts, every other expert is named at most 5 times, and one expert below 64 is named exactly 5 times in the rows of every device.
All inputs are finite; a program needn't handle non-finite values.
Results may differ from the reference program's by a relative error of at most 0.014.
Values may be sent and summed in bfloat16 or wider, within the bound.
No kernel may reach another device: no remote copies, remote signals or barrier semaphores. Data moves between devices by JAX's collectives and lax.ppermute only.
A program may use at most 128 MiB of HBM per device.

```python
import jax
import jax.numpy as jnp
from jax import lax

D = 2048
FF = 768
TOK_DEV = 128
TOP = 2
HOT = 1
COLD = 64
EXPERTS = 65
HOT_LOAD = 32
COLD_SLOTS = 224
CAP = 5
TOKENS = 32768
N_EXPERT = 64
N_DP = 4


def draw_route_ids(key, part):
    blocks = TOKENS // TOK_DEV
    pool_size = COLD * CAP
    key_full, key_rate, key_blocks = jax.random.split(jax.random.fold_in(key, 17), 3)
    full_expert = jax.random.randint(key_full, (), 0, COLD)
    expert_rates = jax.random.randint(key_rate, (COLD,), 0, 64)

    def one_block(block_key):
        key_base, key_order, key_turn = jax.random.split(block_key, 3)
        base_score = jax.random.randint(key_base, (pool_size,), 0, 256)
        slot_ids = jnp.arange(pool_size, dtype=jnp.int32)
        owner_ids = slot_ids // CAP
        slot_level = slot_ids % CAP
        scores = base_score + slot_level * expert_rates[owner_ids]
        scores = scores * pool_size + slot_ids
        scores = jnp.where(owner_ids == full_expert, slot_ids - pool_size, scores)
        neg_best, chosen = lax.top_k(-scores, COLD_SLOTS)
        cold_ids = (chosen // CAP).astype(jnp.int32)
        hot_ids = (COLD + jnp.arange(HOT * HOT_LOAD, dtype=jnp.int32) // HOT_LOAD).astype(jnp.int32)
        listing = jnp.sort(jnp.concatenate([cold_ids, hot_ids]))
        paired = listing.reshape(TOP, TOK_DEV).T
        turns = jax.random.randint(key_turn, (TOK_DEV, 1), 0, TOP)
        columns = (jnp.arange(TOP, dtype=jnp.int32)[None, :] + turns) % TOP
        paired = jnp.take_along_axis(paired, columns, axis=1)
        order = jax.random.permutation(key_order, TOK_DEV)
        return paired[order]
    block_keys = jax.random.split(key_blocks, blocks)
    return jax.vmap(one_block)(block_keys).reshape(TOKENS, TOP).astype(jnp.int32)


def strengthened(array, own_key, source, target, parts, factor):
    owner, partner = [(jnp.arange(array.shape[dim]) // (array.shape[dim] // parts)).reshape([-1 if axis == dim else 1 for axis in range(array.ndim)]) for dim in (source, target)]
    chosen = jax.random.permutation(own_key, parts)[partner]
    strong = (owner == chosen) | (owner == (partner + parts // 2) % parts)
    return jnp.where(strong, factor * array, array)


def block_levels(rng, dims, cuts, least, high):
    level = 1.0
    for dim, blocks in cuts:
        heights = jax.random.uniform(jax.random.fold_in(jax.random.fold_in(rng, 6), dim), (blocks,), jnp.float32, least / len(cuts), high / len(cuts))
        level = level * jnp.repeat(jnp.exp(heights), dims[dim] // blocks).reshape((-1,) + (1,) * (len(dims) - 1 - dim))
    return level


def centred(stream_key, extent, spread, reach, cuts=(), kind=jnp.bfloat16):
    values = jax.random.normal(stream_key, extent, jnp.float32) * spread
    if len(cuts) > 0:
        values = block_levels(stream_key, extent, cuts, -0.22, 0.18) * values
    return jnp.clip(values, min=-reach, max=reach).astype(kind)


def noise_with(stream_key, dims, deviation, bound, pieces, heavy, kind=jnp.bfloat16):
    values = deviation * jax.random.normal(stream_key, dims, jnp.float32)
    if pieces:
        values = values * block_levels(stream_key, dims, pieces, -0.22, 0.18)
    return jnp.clip(strengthened(values, jax.random.fold_in(stream_key, 3), *heavy), -bound, bound).astype(kind)


def setup_inputs(seed: int = 0) -> dict:
    seeds = jax.random.split(jax.random.key(seed), 11)
    tokens = noise_with(seeds[0], (TOKENS, D), 1.0, 24.0, ((0, 256),), (0, 1, 256, 6.0))
    cotangent = centred(seeds[1], (TOKENS, D), 0.5, 3.0, ((0, 256),))
    route_ids = draw_route_ids(jax.random.fold_in(seeds[10], 71), 0)
    route_weights = jnp.clip(0.2 + 0.8 * jax.random.uniform(seeds[3], (TOKENS, TOP), jnp.float32) ** block_levels(seeds[3], (TOKENS, TOP), ((0, 256),), -0.2, 0.2), 0.2, 1.0)
    cold_gate = centred(seeds[4], (COLD, FF, D), D ** -0.5, 0.125, ((0, 64), (1, 4)))
    cold_up = centred(seeds[5], (COLD, FF, D), D ** -0.5, 0.125, ((0, 64), (1, 4)))
    cold_down = centred(seeds[6], (COLD, FF, D), FF ** -0.5, 0.21875, ((0, 64), (1, 4)))
    hot_gate = centred(seeds[7], (HOT, FF, D), D ** -0.5, 0.125, ((1, 4),))
    hot_up = centred(seeds[8], (HOT, FF, D), D ** -0.5, 0.125, ((1, 4),))
    hot_down = centred(seeds[9], (HOT, FF, D), FF ** -0.5, 0.21875, ((1, 4),))
    return {"tokens": tokens, "cotangent": cotangent, "route_ids": route_ids, "route_weights": route_weights, "cold_gate": cold_gate, "cold_up": cold_up, "cold_down": cold_down, "hot_gate": hot_gate, "hot_up": hot_up, "hot_down": hot_down}


def expert_block(rows_x, rows_d, w_gate, w_up, w_down, grouped):
    count = rows_x.shape[0]
    quarter = w_gate.shape[0] // N_DP
    last_pair = (((1,), (1,)), ((), ()))
    pre_gate = lax.dot_general(rows_x, w_gate, last_pair, preferred_element_type=jnp.float32)
    pre_up = lax.dot_general(rows_x, w_up, last_pair, preferred_element_type=jnp.float32)
    sigma = jax.nn.sigmoid(pre_gate)
    act_full = pre_gate * sigma
    slope = sigma * (1.0 + pre_gate * (1.0 - sigma))
    act = (act_full * pre_up).astype(jnp.bfloat16)
    act_q = act.astype(jnp.float32).reshape(count, N_DP, quarter)
    down_q = w_down.astype(jnp.float32).reshape(N_DP, quarter, D)
    out_part = jnp.einsum("rqf,qfd->rqd", act_q, down_q).astype(jnp.bfloat16)
    out_part = lax.optimization_barrier(out_part)
    expert_out = jnp.sum(out_part.astype(jnp.float32), axis=1).astype(jnp.bfloat16)
    d_act = lax.dot_general(rows_d, w_down, last_pair, preferred_element_type=jnp.float32)
    d_gate = (d_act * pre_up * slope).astype(jnp.bfloat16)
    d_up = (d_act * act_full).astype(jnp.bfloat16)
    gate_q = w_gate.astype(jnp.float32).reshape(N_DP, quarter, D)
    up_q = w_up.astype(jnp.float32).reshape(N_DP, quarter, D)
    dg_q = d_gate.astype(jnp.float32).reshape(count, N_DP, quarter)
    du_q = d_up.astype(jnp.float32).reshape(count, N_DP, quarter)
    dx_part = (jnp.einsum("rqf,qfd->rqd", dg_q, gate_q) + jnp.einsum("rqf,qfd->rqd", du_q, up_q)).astype(jnp.bfloat16)
    dx_part = lax.optimization_barrier(dx_part)
    dx_pair = jnp.sum(dx_part.astype(jnp.float32), axis=1).astype(jnp.bfloat16)
    if grouped:
        xs = rows_x.astype(jnp.float32).reshape(N_DP, -1, D)
        ds = rows_d.astype(jnp.float32).reshape(N_DP, -1, D)
        dg = d_gate.astype(jnp.float32).reshape(N_DP, -1, w_gate.shape[0])
        du = d_up.astype(jnp.float32).reshape(N_DP, -1, w_gate.shape[0])
        av = act.astype(jnp.float32).reshape(N_DP, -1, w_gate.shape[0])
        part_gate = jnp.einsum("gpf,gpd->gfd", dg, xs).astype(jnp.bfloat16)
        part_up = jnp.einsum("gpf,gpd->gfd", du, xs).astype(jnp.bfloat16)
        part_down = jnp.einsum("gpf,gpd->gfd", av, ds).astype(jnp.bfloat16)
        part_gate, part_up, part_down = lax.optimization_barrier((part_gate, part_up, part_down))
        grad_gate = jnp.sum(part_gate.astype(jnp.float32), axis=0)
        grad_up = jnp.sum(part_up.astype(jnp.float32), axis=0)
        grad_down = jnp.sum(part_down.astype(jnp.float32), axis=0)
    else:
        grad_gate = jnp.dot(d_gate.T, rows_x, preferred_element_type=jnp.float32)
        grad_up = jnp.dot(d_up.T, rows_x, preferred_element_type=jnp.float32)
        grad_down = jnp.dot(act.T, rows_d, preferred_element_type=jnp.float32)
    return expert_out, dx_pair, grad_gate, grad_up, grad_down


def reference(tokens, cotangent, route_ids, route_weights, cold_gate, cold_up, cold_down, hot_gate, hot_up, hot_down):
    pair_count = TOKENS * TOP
    flat_ids = route_ids.reshape(pair_count).astype(jnp.int32)
    pair_gain = route_weights.reshape(pair_count)
    token_of = (jnp.arange(pair_count, dtype=jnp.int32) // TOP).astype(jnp.int32)
    group_of = ((token_of // TOK_DEV) % N_DP).astype(jnp.int32)
    pair_cot = (pair_gain[:, None] * cotangent[token_of].astype(jnp.float32)).astype(jnp.bfloat16)
    combo = (flat_ids * N_DP + group_of).astype(jnp.int32)
    onehot = (combo[:, None] == jnp.arange(EXPERTS * N_DP, dtype=jnp.int32)[None, :]).astype(jnp.int32)
    slot_rank = jnp.sum((jnp.cumsum(onehot, axis=0) - onehot) * onehot, axis=1).astype(jnp.int32)

    def run_group(first, count, per_group, w_gate, w_up, w_down, grouped):
        buffer = N_DP * per_group
        mine = (flat_ids >= first) & (flat_ids < first + count)
        position = jnp.where(mine, (flat_ids - first) * buffer + group_of * per_group + slot_rank, count * buffer).astype(jnp.int32)
        row_index = jnp.zeros((count * buffer + 1,), jnp.int32).at[position].set(jnp.arange(pair_count, dtype=jnp.int32))
        row_index = row_index[:count * buffer].reshape(count, buffer)
        live_mask = jnp.zeros((count * buffer + 1,), jnp.bool_).at[position].set(True)
        live_mask = live_mask[:count * buffer].reshape(count, buffer)

        def one_expert(expert_item):
            pair_index, live_rows, g_weight, u_weight, d_weight = expert_item
            picked_x = tokens[token_of[pair_index]]
            picked_d = pair_cot[pair_index]
            rows_x = jnp.where(live_rows[:, None], picked_x, jnp.zeros_like(picked_x))
            rows_d = jnp.where(live_rows[:, None], picked_d, jnp.zeros_like(picked_d))
            return expert_block(rows_x, rows_d, g_weight, u_weight, d_weight, grouped)

        results = lax.map(one_expert, (row_index, live_mask, w_gate, w_up, w_down))
        clipped = jnp.minimum(position, count * buffer - 1).astype(jnp.int32)
        outs_pair = results[0].reshape(count * buffer, D)[clipped]
        grads_pair = results[1].reshape(count * buffer, D)[clipped]
        return mine, outs_pair, grads_pair, results[2], results[3], results[4]

    cold_mine, cold_out, cold_dx, cg_grad, cu_grad, cd_grad = run_group(0, COLD, N_EXPERT * CAP, cold_gate, cold_up, cold_down, True)
    hot_mine, hot_out, hot_dx, hg_grad, hu_grad, hd_grad = run_group(COLD, HOT, N_EXPERT * HOT_LOAD, hot_gate, hot_up, hot_down, False)
    expert_out = jnp.where(cold_mine[:, None], cold_out, hot_out).reshape(TOKENS, TOP, D).astype(jnp.float32)
    dx_pair = jnp.where(cold_mine[:, None], cold_dx, hot_dx).reshape(TOKENS, TOP, D).astype(jnp.float32)
    mixed = jnp.sum(route_weights[:, :, None] * expert_out, axis=1).astype(jnp.bfloat16)
    route_grad = jnp.sum(cotangent.astype(jnp.float32)[:, None, :] * expert_out, axis=2)
    token_grad = jnp.sum(dx_pair, axis=1).astype(jnp.bfloat16)
    return (mixed, token_grad, route_grad, cg_grad.astype(jnp.bfloat16), cu_grad.astype(jnp.bfloat16), cd_grad.astype(jnp.bfloat16), hg_grad, hu_grad, hd_grad)
```

```python
import jax
import jax.numpy as jnp
import numpy as np
from jax import lax
from jax.experimental import pallas as pl
from jax.experimental.pallas import tpu as pltpu
from jax.sharding import PartitionSpec as P

F32 = jnp.float32
BF16 = jnp.bfloat16
T = 128
D = 2048
Q = 192
OWN = 64
CAP = 5
SLOTS = OWN * CAP
HOT = 32
NDP = 4
HALF = 3 * Q // 2
CH = 16
PEERS = 8
GROUP = PEERS * CAP
BLOCK = PEERS * CH * CAP
VMEM = 56 * 1024 * 1024


def packing():
    out = np.zeros((BLOCK, BLOCK), np.float32)
    for p in range(PEERS):
        for c in range(CH):
            for s in range(CAP):
                out[p * CH * CAP + c * CAP + s, c * GROUP + p * CAP + s] = 1.0
    return out


def dot(a, b, ca, cb):
    return lax.dot_general(a, b, (((ca,), (cb,)), ((), ())), preferred_element_type=F32)


def diagonal(n):
    return lax.broadcasted_iota(jnp.int32, (n, n), 0) == lax.broadcasted_iota(jnp.int32, (n, n), 1)


def as_row(col):
    return jnp.sum(jnp.where(diagonal(col.shape[0]), col, 0.0), axis=0, keepdims=True)


def as_col(row):
    return jnp.sum(jnp.where(diagonal(row.shape[1]), row, 0.0), axis=1, keepdims=True)


def pair_ids(ids):
    r0, r1 = ids[0:1, :].astype(F32), ids[1:2, :].astype(F32)
    col = jnp.concatenate([as_col(r0), as_col(r1)], axis=0)
    row = jnp.concatenate([r0, r1], axis=1)
    first = lax.broadcasted_iota(jnp.int32, (2 * T, 2 * T), 0)
    second = lax.broadcasted_iota(jnp.int32, (2 * T, 2 * T), 1)
    return col, row, first, second


def slot_of(ident, rank):
    return jnp.where(ident < float(OWN), ident * float(CAP) + rank, float(SLOTS) + rank)


def pack(perm, left, right, out):
    def body(g, carry):
        r0 = pl.multiple_of(g * GROUP, 8)
        pieces = []
        for c in range(CH):
            pieces.append(
                jnp.concatenate(
                    [
                        left[pl.ds(r0, GROUP), c * 128 : (c + 1) * 128],
                        right[pl.ds(r0, GROUP), c * 128 : (c + 1) * 128],
                    ],
                    axis=1,
                )
            )
        rows = jnp.concatenate(pieces, axis=0).astype(BF16)
        out[pl.ds(pl.multiple_of(g * BLOCK, 128), BLOCK), :] = dot(perm[...], rows, 1, 0).astype(BF16)
        return carry

    lax.fori_loop(0, OWN // PEERS, body, 0)


def unpack(perm, src, left, right):
    def body(g, carry):
        r0 = pl.multiple_of(g * GROUP, 8)
        rows = dot(perm[...], src[pl.ds(pl.multiple_of(g * BLOCK, 128), BLOCK), :], 1, 0)
        for c in range(CH):
            left[pl.ds(r0, GROUP), c * 128 : (c + 1) * 128] = rows[c * GROUP : (c + 1) * GROUP, :128]
            right[pl.ds(r0, GROUP), c * 128 : (c + 1) * 128] = rows[c * GROUP : (c + 1) * GROUP, 128:]
        return carry

    lax.fori_loop(0, OWN // PEERS, body, 0)


def dispatch_kernel(tok, cot, ids, gain, perm, send, hot, rx, rd):
    col, row, first, second = pair_ids(ids[...])
    rank = jnp.sum(jnp.where((col == row) & (first < second), 1.0, 0.0), axis=0, keepdims=True)
    target = slot_of(row, rank)
    slot = lax.broadcasted_iota(jnp.int32, (SLOTS + HOT, 2 * T), 0).astype(F32)
    place = jnp.where(slot == target, 1.0, 0.0)
    g = gain[...]
    g_row = jnp.concatenate([g[0:1, :], g[1:2, :]], axis=1)
    g_slot = jnp.sum(place * g_row, axis=1, keepdims=True)
    of_tok = (place[:, :T] + place[:, T:]).astype(BF16)
    for c in range(4):
        cols = slice(c * 512, (c + 1) * 512)
        rx[:, cols] = dot(of_tok, tok[:, cols], 1, 0)
        rd[:, cols] = dot(of_tok, cot[:, cols], 1, 0) * g_slot
    hot[0:HOT, :] = rx[SLOTS:, :].astype(BF16)
    hot[HOT:, :] = rd[SLOTS:, :].astype(BF16)
    pack(perm, rx, rd, send)


def expert_math(x, d, wg, wu, wd):
    return hidden(dot(x, wg, 1, 1), dot(x, wu, 1, 1), dot(d, wd, 1, 1))


def hidden(pre_g, pre_u, d_act):
    sig = 1.0 / (1.0 + jnp.exp(-pre_g))
    silu = pre_g * sig
    act = (silu * pre_u).astype(BF16)
    d_g = (d_act * pre_u * (sig * (1.0 + pre_g * (1.0 - sig)))).astype(BF16)
    d_u = (d_act * silu).astype(BF16)
    return act, d_g, d_u


def hot_kernel(place, rows, wg, wu, wd, p0, p1, p2, p3, keep, give):
    starts = [pl.multiple_of(lax.rem(place[1] + i, NDP) * 2 * HOT, 2 * HOT) for i in (0, 3, 1, 2)]
    x = jnp.concatenate([rows[pl.ds(s, HOT), :] for s in starts], axis=0)
    d = jnp.concatenate([rows[pl.ds(s + HOT, HOT), :] for s in starts], axis=0)
    act, d_g, d_u = expert_math(x, d, wg[0], wu[0], wd[0])
    for c in range(4):
        cols = slice(c * 512, (c + 1) * 512)
        out = dot(act, wd[0, :, cols], 1, 0).astype(BF16)
        dx = (dot(d_g, wg[0, :, cols], 1, 0) + dot(d_u, wu[0, :, cols], 1, 0)).astype(BF16)
        for r, part in enumerate((p0, p1, p2, p3)):
            part[0:HOT, cols] = out[r * HOT : (r + 1) * HOT]
            part[HOT:, cols] = dx[r * HOT : (r + 1) * HOT]
    mine = place[0] == 0
    both = jnp.concatenate([d_g, d_u], axis=1)
    for c in range(8):
        cols = slice(c * 256, (c + 1) * 256)
        gu = dot(x[:, cols], both, 0, 0).reshape(4, 2, 32, 2 * Q)
        dn = dot(d[:, cols], act, 0, 0).reshape(4, 2, 32, Q)
        for i in range(4):
            base = (c * 4 + i) * 48
            for dst, low in ((keep, mine), (give, jnp.logical_not(mine))):
                dst[base : base + 32, :] = jnp.where(low, gu[i, 0], gu[i, 1])
                pick = jnp.where(low, dn[i, 0], dn[i, 1])
                dst[base + 32 : base + 48, :] = jnp.concatenate([pick[:16], pick[16:]], axis=1)


def fill(parts, wg, wu, wd, at, sems, i):
    gate, u, rest = parts
    return [
        pltpu.make_async_copy(gate, wg.at[at : at + Q, :], sems.at[i]),
        pltpu.make_async_copy(u, wu.at[at : at + Q // 2, :], sems.at[i + 1]),
        pltpu.make_async_copy(rest.at[0 : Q // 2, :], wu.at[at + Q // 2 : at + Q, :], sems.at[i + 2]),
        pltpu.make_async_copy(rest.at[Q // 2 : HALF, :], wd.at[at : at + Q, :], sems.at[i + 3]),
    ]


def far_kernel(rows, perm, gate, u, rest, x_out, d_out, hid, g_gate, g_u, g_v, g_down, xf, df):
    unpack(perm, rows, xf, df)
    x_out[...] = xf[...].astype(BF16)
    d_out[...] = df[...].astype(BF16)
    wu = jnp.concatenate([u[...], rest[0 : Q // 2, :]], axis=0)
    act, d_g, d_u = expert_math(x_out[...], d_out[...], gate[...], wu, rest[Q // 2 : HALF, :])
    hid[0, :, :] = act
    hid[1, :, :] = d_g
    hid[2, :, :] = d_u
    both = jnp.concatenate([d_g, d_u], axis=1)
    for c in range(4):
        cols = slice(c * 512, (c + 1) * 512)
        gu = dot(both, x_out[:, cols], 0, 0).astype(BF16)
        g_down[:, cols] = dot(act, d_out[:, cols], 0, 0).astype(BF16)
        g_gate[:, cols] = gu[0:Q]
        g_u[:, cols] = gu[Q:HALF]
        g_v[:, cols] = gu[HALF:]


def near_kernel(x, d, hid, perm, *refs):
    parts, (back, mine, wg, wu, wd, of, df, sems) = refs[:12], refs[12:]
    copies = []
    for i in range(NDP):
        copies += fill(parts[3 * i : 3 * i + 3], wg, wu, wd, i * Q, sems, 4 * i)
    for k in range(4):
        for i in range(0, 16, 4):
            copies[i + k].start()
    n = 3 * Q
    for i in range(0, 16, 4):
        copies[i].wait()
    pre_g = dot(x[...], wg[0:n, :], 1, 1)
    for i in range(0, 16, 4):
        copies[i + 1].wait()
        copies[i + 2].wait()
    pre_u = dot(x[...], wu[0:n, :], 1, 1)
    for i in range(0, 16, 4):
        copies[i + 3].wait()
    d_act = dot(d[...], wd[0:n, :], 1, 1)
    act, d_g, d_u = hidden(pre_g, pre_u, d_act)
    mine[0, :, :] = act
    mine[1, :, :] = d_g
    mine[2, :, :] = d_u
    act = jnp.concatenate([act, hid[0]], axis=1)
    d_g = jnp.concatenate([d_g, hid[1]], axis=1)
    d_u = jnp.concatenate([d_u, hid[2]], axis=1)
    for c in range(4):
        cols = slice(c * 512, (c + 1) * 512)
        of[:, cols] = dot(act, wd[:, cols], 1, 0)
        df[:, cols] = dot(d_g, wg[:, cols], 1, 0) + dot(d_u, wu[:, cols], 1, 0)
    pack(perm, of, df, back)


def grad_kernel(x, d, mine, *outs):
    for s in range(3):
        low, up = outs[2 * s], outs[2 * s + 1]
        at = slice(s * Q, (s + 1) * Q)
        act = mine[0, :, at]
        both = jnp.concatenate([mine[1, :, at], mine[2, :, at]], axis=1)
        for c in range(4):
            cols = slice(c * 512, (c + 1) * 512)
            gu = dot(both, x[:, cols], 0, 0).astype(BF16)
            low[:, cols] = gu[0:HALF]
            up[0 : Q // 2, cols] = gu[HALF:]
            up[Q // 2 :, cols] = dot(act, d[:, cols], 0, 0).astype(BF16)


def finish_kernel(a_low, a_up, b_low, b_up, c_low, c_up, gate, up, down):
    low = (a_low[...].astype(F32) + b_low[...].astype(F32) + c_low[...].astype(F32)).astype(BF16)
    top = (a_up[...].astype(F32) + b_up[...].astype(F32) + c_up[...].astype(F32)).astype(BF16)
    gate[0] = low[0:Q]
    up[0, 0 : Q // 2, :] = low[Q:]
    up[0, Q // 2 :, :] = top[0 : Q // 2]
    down[0] = top[Q // 2 :]


def combine_kernel(back, h0, h1, h2, h3, cot, ids, gain, perm, mixed, tgrad, rgrad, of, df):
    unpack(perm, back, of, df)
    hot = h0[...].astype(F32) + h1[...].astype(F32) + h2[...].astype(F32) + h3[...].astype(F32)
    of[SLOTS:, :] = hot[0:HOT, :]
    df[SLOTS:, :] = hot[HOT:, :]
    col, row, first, second = pair_ids(ids[...])
    rank = jnp.sum(jnp.where((col == row) & (second < first), 1.0, 0.0), axis=1, keepdims=True)
    target = slot_of(col, rank)
    slot = lax.broadcasted_iota(jnp.int32, (2 * T, SLOTS + HOT), 1).astype(F32)
    place = jnp.where(slot == target, 1.0, 0.0)
    p0, p1 = place[:T].astype(BF16), place[T:].astype(BF16)
    both = (place[:T] + place[T:]).astype(BF16)
    g0, g1 = as_col(gain[0:1, :]), as_col(gain[1:2, :])
    r0 = jnp.zeros((T, 1), F32)
    r1 = jnp.zeros((T, 1), F32)
    for c in range(4):
        cols = slice(c * 512, (c + 1) * 512)
        o = of[:, cols].astype(BF16)
        e0, e1 = dot(p0, o, 1, 0), dot(p1, o, 1, 0)
        ct = cot[:, cols].astype(F32)
        mixed[:, cols] = (g0 * e0 + g1 * e1).astype(BF16)
        r0 = r0 + jnp.sum(ct * e0, axis=1, keepdims=True)
        r1 = r1 + jnp.sum(ct * e1, axis=1, keepdims=True)
        tgrad[:, cols] = dot(both, df[:, cols].astype(BF16), 1, 0).astype(BF16)
    rgrad[0:1, :] = as_row(r0)
    rgrad[1:2, :] = as_row(r1)


def params(**kw):
    return pltpu.CompilerParams(vmem_limit_bytes=VMEM, **kw)


def cost(flops, nbytes):
    return pl.CostEstimate(flops=int(flops), bytes_accessed=int(nbytes), transcendentals=0)


VM = pl.BlockSpec(memory_space=pltpu.VMEM)


def local(tokens, cotangent, route_ids, route_weights, cold_gate, cold_up, cold_down, hot_gate, hot_up, hot_down):
    perm = jnp.asarray(packing(), BF16)
    perm_t = jnp.asarray(packing().T, BF16)
    ids_t, gain_t = route_ids.T, route_weights.T
    expert = lax.axis_index("expert")
    place = jnp.stack([lax.rem(expert, 2), lax.axis_index("dp")])

    right = [(i, (i + 1) % NDP) for i in range(NDP)]
    left = [(i, (i - 1) % NDP) for i in range(NDP)]
    own_gate, own_u = cold_gate[0], cold_up[0, : Q // 2]
    own_rest = jnp.concatenate([cold_up[0, Q // 2 :], cold_down[0]], axis=0)
    l_u = lax.ppermute(own_u, "dp", right)
    r_u = lax.ppermute(own_u, "dp", left)
    l_gate = lax.ppermute(own_gate, "dp", right)
    r_gate = lax.ppermute(own_gate, "dp", left)
    l_rest = lax.ppermute(own_rest, "dp", right)
    r_rest = lax.ppermute(own_rest, "dp", left)
    f_u = lax.ppermute(l_u, "dp", right)
    f_gate = lax.ppermute(l_gate, "dp", right)
    f_rest = lax.ppermute(r_rest, "dp", left)

    send, hot_rows = pl.pallas_call(
        dispatch_kernel,
        out_shape=(
            jax.ShapeDtypeStruct((OWN * CH * CAP, 256), BF16),
            jax.ShapeDtypeStruct((2 * HOT, D), BF16),
        ),
        in_specs=[VM] * 5,
        out_specs=(VM, VM),
        scratch_shapes=[pltpu.VMEM((SLOTS + HOT, D), F32), pltpu.VMEM((SLOTS + HOT, D), F32)],
        compiler_params=params(),
        cost_estimate=cost(4e9, 6e6),
    )(tokens, cotangent, ids_t, gain_t, perm)

    far = [(i, (i + 2) % NDP) for i in range(NDP)]
    hot_all = lax.all_gather(hot_rows, "dp", axis=0, tiled=True)
    send = lax.optimization_barrier((send, l_u, r_u))[0]
    arrived = lax.all_to_all(
        send.reshape(OWN, CH * CAP, 256), "expert", split_axis=0, concat_axis=0, tiled=True
    ).reshape(OWN * CH * CAP, 256)

    hot_all = lax.optimization_barrier((hot_all, l_u, r_u, l_gate, r_gate, l_rest, r_rest))[0]
    hot_own, to_l, to_r, to_f, keep, give = pl.pallas_call(
        hot_kernel,
        out_shape=(
            jax.ShapeDtypeStruct((2 * HOT, D), BF16),
            jax.ShapeDtypeStruct((2 * HOT, D), BF16),
            jax.ShapeDtypeStruct((2 * HOT, D), BF16),
            jax.ShapeDtypeStruct((2 * HOT, D), BF16),
            jax.ShapeDtypeStruct((OWN // 2 * 48, 2 * Q), F32),
            jax.ShapeDtypeStruct((OWN // 2 * 48, 2 * Q), F32),
        ),
        in_specs=[pl.BlockSpec(memory_space=pltpu.SMEM)] + [VM] * 4,
        out_specs=(VM,) * 6,
        compiler_params=params(),
        cost_estimate=cost(1e9, 9e6),
    )(place, hot_all, hot_gate, hot_up, hot_down)
    give = lax.optimization_barrier((give, f_u, f_gate, f_rest))[0]
    back_r = lax.ppermute(to_l, "dp", left)
    back_l = lax.ppermute(to_r, "dp", right)
    back_f = lax.ppermute(to_f, "dp", far)
    came = lax.ppermute(give, "expert", [(i, i ^ 1) for i in range(OWN)])
    along_y = [[y * 16 + r for y in range(4)] for r in range(16)]
    along_z = [[y * 16 + z * 2 + c for z in range(8)] for y in range(4) for c in range(2)]
    hot_y = lax.psum_scatter(keep + came, "expert", scatter_dimension=0, axis_index_groups=along_y, tiled=True)
    half = jax.ShapeDtypeStruct((HALF, D), BF16)
    x, d, hid, gf_gate, gf_u, gf_v, gf_down = pl.pallas_call(
        far_kernel,
        out_shape=(
            jax.ShapeDtypeStruct((SLOTS, D), BF16),
            jax.ShapeDtypeStruct((SLOTS, D), BF16),
            jax.ShapeDtypeStruct((3, SLOTS, Q), BF16),
            jax.ShapeDtypeStruct((Q, D), BF16),
            jax.ShapeDtypeStruct((Q // 2, D), BF16),
            jax.ShapeDtypeStruct((Q // 2, D), BF16),
            jax.ShapeDtypeStruct((Q, D), BF16),
        ),
        in_specs=[VM] * 5,
        out_specs=(VM,) * 7,
        scratch_shapes=[pltpu.VMEM((SLOTS, D), F32), pltpu.VMEM((SLOTS, D), F32)],
        compiler_params=params(),
        cost_estimate=cost(4e9, 12e6),
    )(arrived, perm_t, f_gate, f_u, f_rest)
    gf_gate, gf_down, back_r, back_l, back_f = lax.optimization_barrier((gf_gate, gf_down, back_r, back_l, back_f))
    came_gate = lax.ppermute(gf_gate, "dp", right)
    came_down = lax.ppermute(gf_down, "dp", left)
    came_u = lax.ppermute(gf_u, "dp", right)
    came_v = lax.ppermute(gf_v, "dp", left)
    hbm = pl.BlockSpec(memory_space=pl.ANY)
    back, mine = pl.pallas_call(
        near_kernel,
        out_shape=(
            jax.ShapeDtypeStruct((OWN * CH * CAP, 256), BF16),
            jax.ShapeDtypeStruct((3, SLOTS, 3 * Q), BF16),
        ),
        in_specs=[VM] * 4 + [hbm] * 12,
        out_specs=(VM, VM),
        scratch_shapes=[
            pltpu.VMEM((NDP * Q, D), BF16),
            pltpu.VMEM((NDP * Q, D), BF16),
            pltpu.VMEM((NDP * Q, D), BF16),
            pltpu.VMEM((SLOTS, D), F32),
            pltpu.VMEM((SLOTS, D), F32),
            pltpu.SemaphoreType.DMA((16,)),
        ],
        compiler_params=params(),
        cost_estimate=cost(1e6, 1e5),
    )(x, d, hid, perm, own_gate, own_u, own_rest, l_gate, l_u, l_rest, r_gate, r_u, r_rest, f_gate, f_u, f_rest)
    go_low, go_up, gl_low, gl_up, gr_low, gr_up = pl.pallas_call(
        grad_kernel,
        out_shape=(half,) * 6,
        in_specs=[VM] * 3,
        out_specs=(VM,) * 6,
        compiler_params=params(),
        cost_estimate=cost(1e6, 1e5),
    )(x, d, mine)

    def plus(a, *b):
        return (a.astype(F32) + jnp.concatenate(b, axis=0).astype(F32)).astype(BF16)

    a_up = lax.ppermute(gr_up, "dp", right)
    b_low = lax.ppermute(gl_low, "dp", left)
    a_low = lax.ppermute(plus(gr_low, came_gate, came_u), "dp", right)
    b_up = lax.ppermute(plus(gl_up, came_v, came_down), "dp", left)
    back = lax.optimization_barrier((back, came_gate, came_down))[0]
    returned = lax.all_to_all(
        back.reshape(OWN, CH * CAP, 256), "expert", split_axis=0, concat_axis=0, tiled=True
    ).reshape(OWN * CH * CAP, 256)

    hot_z = lax.psum_scatter(hot_y, "expert", scatter_dimension=0, axis_index_groups=along_z, tiled=True)
    hot_low = hot_z[0:32].T
    hot_up_part = jnp.concatenate([hot_z[32:, :Q], hot_z[32:, Q:]], axis=0).T

    mixed, token_grad, route_grad = pl.pallas_call(
        combine_kernel,
        out_shape=(
            jax.ShapeDtypeStruct((T, D), BF16),
            jax.ShapeDtypeStruct((T, D), BF16),
            jax.ShapeDtypeStruct((2, T), F32),
        ),
        in_specs=[VM] * 9,
        out_specs=(VM, VM, VM),
        scratch_shapes=[pltpu.VMEM((SLOTS + HOT, D), F32), pltpu.VMEM((SLOTS + HOT, D), F32)],
        compiler_params=params(),
        cost_estimate=cost(4e9, 6e6),
    )(returned, hot_own, back_r, back_l, back_f, cotangent, ids_t, gain_t, perm_t)
    third = jax.ShapeDtypeStruct((1, Q, D), BF16)
    a_low, mixed = lax.optimization_barrier((a_low, mixed))
    gate_grad, up_grad, down_grad = pl.pallas_call(
        finish_kernel,
        out_shape=(third,) * 3,
        grid=(4,),
        in_specs=[pl.BlockSpec((HALF, D // 4), lambda i: (0, i))] * 6,
        out_specs=(pl.BlockSpec((1, Q, D // 4), lambda i: (0, 0, i)),) * 3,
        compiler_params=params(),
        cost_estimate=cost(1e6, 10e6),
    )(go_low, go_up, a_low, a_up, b_low, b_up)
    return (
        mixed,
        token_grad,
        route_grad.T,
        gate_grad,
        up_grad,
        down_grad,
        hot_low[None, 0:Q],
        hot_low[None, Q:],
        hot_up_part[None],
    )


def solution(mesh):
    rows = P(("expert", "dp"), None)
    cold = P("expert", "dp", None)
    hot = P(None, "dp", None)
    split = P(None, "dp", "expert")
    return jax.shard_map(
        local,
        mesh=mesh,
        in_specs=(rows, rows, rows, rows, cold, cold, cold, hot, hot, hot),
        out_specs=(rows, rows, rows, cold, cold, cold, split, split, split),
        check_vma=False,
    )
```

```python
import jax
import jax.numpy as jnp
import numpy as np
from jax import lax
from jax.experimental import pallas as pl
from jax.experimental.pallas import tpu as pltpu
from jax.sharding import PartitionSpec as P

F32 = jnp.float32
BF16 = jnp.bfloat16
T = 128
D = 2048
Q = 192
OWN = 64
CAP = 5
SLOTS = OWN * CAP
HOT = 32
NDP = 4
HALF = 3 * Q // 2
CH = 16
PEERS = 8
GROUP = PEERS * CAP
BLOCK = PEERS * CH * CAP
VMEM = 56 * 1024 * 1024


def packing():
    out = np.zeros((BLOCK, BLOCK), np.float32)
    for p in range(PEERS):
        for c in range(CH):
            for s in range(CAP):
                out[p * CH * CAP + c * CAP + s, c * GROUP + p * CAP + s] = 1.0
    return out


def dot(a, b, ca, cb):
    return lax.dot_general(a, b, (((ca,), (cb,)), ((), ())), preferred_element_type=F32)


def diagonal(n):
    return lax.broadcasted_iota(jnp.int32, (n, n), 0) == lax.broadcasted_iota(jnp.int32, (n, n), 1)


def as_row(col):
    return jnp.sum(jnp.where(diagonal(col.shape[0]), col, 0.0), axis=0, keepdims=True)


def as_col(row):
    return jnp.sum(jnp.where(diagonal(row.shape[1]), row, 0.0), axis=1, keepdims=True)


def pair_ids(ids):
    r0, r1 = ids[0:1, :].astype(F32), ids[1:2, :].astype(F32)
    col = jnp.concatenate([as_col(r0), as_col(r1)], axis=0)
    row = jnp.concatenate([r0, r1], axis=1)
    first = lax.broadcasted_iota(jnp.int32, (2 * T, 2 * T), 0)
    second = lax.broadcasted_iota(jnp.int32, (2 * T, 2 * T), 1)
    return col, row, first, second


def slot_of(ident, rank):
    return jnp.where(ident < float(OWN), ident * float(CAP) + rank, float(SLOTS) + rank)


def pack(perm, left, right, out):
    def body(g, carry):
        r0 = pl.multiple_of(g * GROUP, 8)
        pieces = []
        for c in range(CH):
            pieces.append(
                jnp.concatenate(
                    [
                        left[pl.ds(r0, GROUP), c * 128 : (c + 1) * 128],
                        right[pl.ds(r0, GROUP), c * 128 : (c + 1) * 128],
                    ],
                    axis=1,
                )
            )
        rows = jnp.concatenate(pieces, axis=0).astype(BF16)
        out[pl.ds(pl.multiple_of(g * BLOCK, 128), BLOCK), :] = dot(perm[...], rows, 1, 0).astype(BF16)
        return carry

    lax.fori_loop(0, OWN // PEERS, body, 0, unroll=True)


def unpack(perm, src, left, right):
    def body(g, carry):
        r0 = pl.multiple_of(g * GROUP, 8)
        rows = dot(perm[...], src[pl.ds(pl.multiple_of(g * BLOCK, 128), BLOCK), :], 1, 0)
        for c in range(CH):
            left[pl.ds(r0, GROUP), c * 128 : (c + 1) * 128] = rows[c * GROUP : (c + 1) * GROUP, :128]
            right[pl.ds(r0, GROUP), c * 128 : (c + 1) * 128] = rows[c * GROUP : (c + 1) * GROUP, 128:]
        return carry

    lax.fori_loop(0, OWN // PEERS, body, 0, unroll=True)


def dispatch_kernel(tok, cot, ids, gain, perm, send, hot, rx, rd):
    col, row, first, second = pair_ids(ids[...])
    rank = jnp.sum(jnp.where((col == row) & (first < second), 1.0, 0.0), axis=0, keepdims=True)
    target = slot_of(row, rank)
    slot = lax.broadcasted_iota(jnp.int32, (SLOTS + HOT, 2 * T), 0).astype(F32)
    place = jnp.where(slot == target, 1.0, 0.0)
    g = gain[...]
    g_row = jnp.concatenate([g[0:1, :], g[1:2, :]], axis=1)
    g_slot = jnp.sum(place * g_row, axis=1, keepdims=True)
    of_tok = (place[:, :T] + place[:, T:]).astype(BF16)
    for c in range(4):
        cols = slice(c * 512, (c + 1) * 512)
        rx[:, cols] = dot(of_tok, tok[:, cols], 1, 0)
        rd[:, cols] = dot(of_tok, cot[:, cols], 1, 0) * g_slot
    hot[0:HOT, :] = rx[SLOTS:, :].astype(BF16)
    hot[HOT:, :] = rd[SLOTS:, :].astype(BF16)
    pack(perm, rx, rd, send)


def expert_math(x, d, wg, wu, wd):
    return hidden(dot(x, wg, 1, 1), dot(x, wu, 1, 1), dot(d, wd, 1, 1))


def hidden(pre_g, pre_u, d_act):
    sig = 1.0 / (1.0 + jnp.exp(-pre_g))
    silu = pre_g * sig
    act = (silu * pre_u).astype(BF16)
    d_g = (d_act * pre_u * (sig * (1.0 + pre_g * (1.0 - sig)))).astype(BF16)
    d_u = (d_act * silu).astype(BF16)
    return act, d_g, d_u


def hot_kernel(place, rows, wg, wu, wd, p0, p1, p2, p3, keep, give):
    starts = [pl.multiple_of(lax.rem(place[1] + i, NDP) * 2 * HOT, 2 * HOT) for i in (0, 3, 1, 2)]
    x = jnp.concatenate([rows[pl.ds(s, HOT), :] for s in starts], axis=0)
    d = jnp.concatenate([rows[pl.ds(s + HOT, HOT), :] for s in starts], axis=0)
    act, d_g, d_u = expert_math(x, d, wg[0], wu[0], wd[0])
    for c in range(4):
        cols = slice(c * 512, (c + 1) * 512)
        out = dot(act, wd[0, :, cols], 1, 0).astype(BF16)
        dx = (dot(d_g, wg[0, :, cols], 1, 0) + dot(d_u, wu[0, :, cols], 1, 0)).astype(BF16)
        for r, part in enumerate((p0, p1, p2, p3)):
            part[0:HOT, cols] = out[r * HOT : (r + 1) * HOT]
            part[HOT:, cols] = dx[r * HOT : (r + 1) * HOT]
    mine = place[0] == 0
    both = jnp.concatenate([d_g, d_u], axis=1)
    for c in range(8):
        cols = slice(c * 256, (c + 1) * 256)
        gu = dot(x[:, cols], both, 0, 0).reshape(4, 2, 32, 2 * Q)
        dn = dot(d[:, cols], act, 0, 0).reshape(4, 2, 32, Q)
        for i in range(4):
            base = (c * 4 + i) * 48
            for dst, low in ((keep, mine), (give, jnp.logical_not(mine))):
                dst[base : base + 32, :] = jnp.where(low, gu[i, 0], gu[i, 1])
                pick = jnp.where(low, dn[i, 0], dn[i, 1])
                dst[base + 32 : base + 48, :] = jnp.concatenate([pick[:16], pick[16:]], axis=1)


def fill(parts, wg, wu, wd, at, sems, i):
    low, up = parts
    return [
        pltpu.make_async_copy(low.at[0:Q, :], wg.at[at : at + Q, :], sems.at[i]),
        pltpu.make_async_copy(low.at[Q:HALF, :], wu.at[at : at + Q // 2, :], sems.at[i + 1]),
        pltpu.make_async_copy(up.at[0 : Q // 2, :], wu.at[at + Q // 2 : at + Q, :], sems.at[i + 2]),
        pltpu.make_async_copy(up.at[Q // 2 : HALF, :], wd.at[at : at + Q, :], sems.at[i + 3]),
    ]


def far_kernel(rows, perm, low, up, x_out, d_out, hid, g_gate, g_u, g_v, g_down, xf, df):
    unpack(perm, rows, xf, df)
    x_out[...] = xf[...].astype(BF16)
    d_out[...] = df[...].astype(BF16)
    wu = jnp.concatenate([low[Q:HALF, :], up[0 : Q // 2, :]], axis=0)
    act, d_g, d_u = expert_math(x_out[...], d_out[...], low[0:Q, :], wu, up[Q // 2 : HALF, :])
    hid[0, :, :] = act
    hid[1, :, :] = d_g
    hid[2, :, :] = d_u
    both = jnp.concatenate([d_g, d_u], axis=1)
    for c in range(4):
        cols = slice(c * 512, (c + 1) * 512)
        gu = dot(both, x_out[:, cols], 0, 0).astype(BF16)
        g_down[:, cols] = dot(act, d_out[:, cols], 0, 0).astype(BF16)
        g_gate[:, cols] = gu[0:Q]
        g_u[:, cols] = gu[Q:HALF]
        g_v[:, cols] = gu[HALF:]


def near_kernel(x, d, hid, perm, *refs):
    whole, far, (back, mine, wg, wu, wd, of, df, sems) = refs[:3], refs[3:5], refs[5:]
    copies = []
    for i, src in enumerate(whole):
        copies += fill((src.at[0:HALF, :], src.at[HALF : 3 * Q, :]), wg, wu, wd, i * Q, sems, 4 * i)
    copies += fill(far, wg, wu, wd, 3 * Q, sems, 12)
    for k in range(4):
        for i in range(0, 16, 4):
            copies[i + k].start()
    n = 3 * Q
    for i in range(0, 16, 4):
        copies[i].wait()
    pre_g = dot(x[...], wg[0:n, :], 1, 1)
    for i in range(0, 16, 4):
        copies[i + 1].wait()
        copies[i + 2].wait()
    pre_u = dot(x[...], wu[0:n, :], 1, 1)
    for i in range(0, 16, 4):
        copies[i + 3].wait()
    d_act = dot(d[...], wd[0:n, :], 1, 1)
    act, d_g, d_u = hidden(pre_g, pre_u, d_act)
    mine[0, :, :] = act
    mine[1, :, :] = d_g
    mine[2, :, :] = d_u
    act = jnp.concatenate([act, hid[0]], axis=1)
    d_g = jnp.concatenate([d_g, hid[1]], axis=1)
    d_u = jnp.concatenate([d_u, hid[2]], axis=1)
    for c in range(4):
        cols = slice(c * 512, (c + 1) * 512)
        of[:, cols] = dot(act, wd[:, cols], 1, 0)
        df[:, cols] = dot(d_g, wg[:, cols], 1, 0) + dot(d_u, wu[:, cols], 1, 0)
    pack(perm, of, df, back)


def grad_kernel(x, d, mine, *outs):
    for s in range(3):
        low, up = outs[2 * s], outs[2 * s + 1]
        at = slice(s * Q, (s + 1) * Q)
        act = mine[0, :, at]
        both = jnp.concatenate([mine[1, :, at], mine[2, :, at]], axis=1)
        for c in range(4):
            cols = slice(c * 512, (c + 1) * 512)
            gu = dot(both, x[:, cols], 0, 0).astype(BF16)
            low[:, cols] = gu[0:HALF]
            up[0 : Q // 2, cols] = gu[HALF:]
            up[Q // 2 :, cols] = dot(act, d[:, cols], 0, 0).astype(BF16)


def finish_kernel(a_low, a_up, b_low, b_up, c_low, c_up, gate, up, down):
    low = (a_low[...].astype(F32) + b_low[...].astype(F32) + c_low[...].astype(F32)).astype(BF16)
    top = (a_up[...].astype(F32) + b_up[...].astype(F32) + c_up[...].astype(F32)).astype(BF16)
    gate[0] = low[0:Q]
    up[0, 0 : Q // 2, :] = low[Q:]
    up[0, Q // 2 :, :] = top[0 : Q // 2]
    down[0] = top[Q // 2 :]


def combine_kernel(back, h0, h1, h2, h3, cot, ids, gain, perm, mixed, tgrad, rgrad, of, df):
    unpack(perm, back, of, df)
    hot = h0[...].astype(F32) + h1[...].astype(F32) + h2[...].astype(F32) + h3[...].astype(F32)
    of[SLOTS:, :] = hot[0:HOT, :]
    df[SLOTS:, :] = hot[HOT:, :]
    col, row, first, second = pair_ids(ids[...])
    rank = jnp.sum(jnp.where((col == row) & (second < first), 1.0, 0.0), axis=1, keepdims=True)
    target = slot_of(col, rank)
    slot = lax.broadcasted_iota(jnp.int32, (2 * T, SLOTS + HOT), 1).astype(F32)
    place = jnp.where(slot == target, 1.0, 0.0)
    p0, p1 = place[:T].astype(BF16), place[T:].astype(BF16)
    both = (place[:T] + place[T:]).astype(BF16)
    g0, g1 = as_col(gain[0:1, :]), as_col(gain[1:2, :])
    r0 = jnp.zeros((T, 1), F32)
    r1 = jnp.zeros((T, 1), F32)
    for c in range(4):
        cols = slice(c * 512, (c + 1) * 512)
        o = of[:, cols].astype(BF16)
        e0, e1 = dot(p0, o, 1, 0), dot(p1, o, 1, 0)
        ct = cot[:, cols].astype(F32)
        mixed[:, cols] = (g0 * e0 + g1 * e1).astype(BF16)
        r0 = r0 + jnp.sum(ct * e0, axis=1, keepdims=True)
        r1 = r1 + jnp.sum(ct * e1, axis=1, keepdims=True)
        tgrad[:, cols] = dot(both, df[:, cols].astype(BF16), 1, 0).astype(BF16)
    rgrad[0:1, :] = as_row(r0)
    rgrad[1:2, :] = as_row(r1)


def params(**kw):
    return pltpu.CompilerParams(vmem_limit_bytes=VMEM, **kw)


def cost(flops, nbytes):
    return pl.CostEstimate(flops=int(flops), bytes_accessed=int(nbytes), transcendentals=0)


VM = pl.BlockSpec(memory_space=pltpu.VMEM)


def local(tokens, cotangent, route_ids, route_weights, cold_gate, cold_up, cold_down, hot_gate, hot_up, hot_down):
    perm = jnp.asarray(packing(), BF16)
    perm_t = jnp.asarray(packing().T, BF16)
    ids_t, gain_t = route_ids.T, route_weights.T
    expert = lax.axis_index("expert")
    place = jnp.stack([lax.rem(expert, 2), lax.axis_index("dp")])

    right = [(i, (i + 1) % NDP) for i in range(NDP)]
    left = [(i, (i - 1) % NDP) for i in range(NDP)]
    own = jnp.concatenate([cold_gate[0], cold_up[0], cold_down[0]], axis=0)
    from_left = lax.ppermute(own, "dp", right)
    from_right = lax.ppermute(own, "dp", left)
    f_low = lax.ppermute(from_left[:HALF], "dp", right)
    f_up = lax.ppermute(from_right[HALF:], "dp", left)
    tokens, _ = lax.optimization_barrier((tokens, own))

    send, hot_rows = pl.pallas_call(
        dispatch_kernel,
        out_shape=(
            jax.ShapeDtypeStruct((OWN * CH * CAP, 256), BF16),
            jax.ShapeDtypeStruct((2 * HOT, D), BF16),
        ),
        in_specs=[VM] * 5,
        out_specs=(VM, VM),
        scratch_shapes=[pltpu.VMEM((SLOTS + HOT, D), F32), pltpu.VMEM((SLOTS + HOT, D), F32)],
        compiler_params=params(),
        cost_estimate=cost(4e9, 6e6),
    )(tokens, cotangent, ids_t, gain_t, perm)

    far = [(i, (i + 2) % NDP) for i in range(NDP)]
    hot_all = lax.all_gather(hot_rows, "dp", axis=0, tiled=True)
    arrived = lax.all_to_all(
        send.reshape(OWN, CH * CAP, 256), "expert", split_axis=0, concat_axis=0, tiled=True
    ).reshape(OWN * CH * CAP, 256)

    hot_all = lax.optimization_barrier((hot_all, from_left, from_right))[0]
    hot_own, to_l, to_r, to_f, keep, give = pl.pallas_call(
        hot_kernel,
        out_shape=(
            jax.ShapeDtypeStruct((2 * HOT, D), BF16),
            jax.ShapeDtypeStruct((2 * HOT, D), BF16),
            jax.ShapeDtypeStruct((2 * HOT, D), BF16),
            jax.ShapeDtypeStruct((2 * HOT, D), BF16),
            jax.ShapeDtypeStruct((OWN // 2 * 48, 2 * Q), F32),
            jax.ShapeDtypeStruct((OWN // 2 * 48, 2 * Q), F32),
        ),
        in_specs=[pl.BlockSpec(memory_space=pltpu.SMEM)] + [VM] * 4,
        out_specs=(VM,) * 6,
        compiler_params=params(),
        cost_estimate=cost(1e9, 9e6),
    )(place, hot_all, hot_gate, hot_up, hot_down)
    back_r = lax.ppermute(to_l, "dp", left)
    back_l = lax.ppermute(to_r, "dp", right)
    back_f = lax.ppermute(to_f, "dp", far)
    came = lax.ppermute(give, "expert", [(i, i ^ 1) for i in range(OWN)])
    keep, came, _, _ = lax.optimization_barrier((keep, came, f_low, f_up))
    along_y = [[y * 16 + r for y in range(4)] for r in range(16)]
    along_z = [[y * 16 + z * 2 + c for z in range(8)] for y in range(4) for c in range(2)]
    hot_y = lax.psum_scatter(keep + came, "expert", scatter_dimension=0, axis_index_groups=along_y, tiled=True)
    half = jax.ShapeDtypeStruct((HALF, D), BF16)
    x, d, hid, gf_gate, gf_u, gf_v, gf_down = pl.pallas_call(
        far_kernel,
        out_shape=(
            jax.ShapeDtypeStruct((SLOTS, D), BF16),
            jax.ShapeDtypeStruct((SLOTS, D), BF16),
            jax.ShapeDtypeStruct((3, SLOTS, Q), BF16),
            jax.ShapeDtypeStruct((Q, D), BF16),
            jax.ShapeDtypeStruct((Q // 2, D), BF16),
            jax.ShapeDtypeStruct((Q // 2, D), BF16),
            jax.ShapeDtypeStruct((Q, D), BF16),
        ),
        in_specs=[VM] * 4,
        out_specs=(VM,) * 7,
        scratch_shapes=[pltpu.VMEM((SLOTS, D), F32), pltpu.VMEM((SLOTS, D), F32)],
        compiler_params=params(),
        cost_estimate=cost(4e9, 12e6),
    )(arrived, perm_t, f_low, f_up)
    came_gate = lax.ppermute(gf_gate, "dp", right)
    came_down = lax.ppermute(gf_down, "dp", left)
    came_u = lax.ppermute(gf_u, "dp", right)
    came_v = lax.ppermute(gf_v, "dp", left)
    hbm = pl.BlockSpec(memory_space=pl.ANY)
    back, mine = pl.pallas_call(
        near_kernel,
        out_shape=(
            jax.ShapeDtypeStruct((OWN * CH * CAP, 256), BF16),
            jax.ShapeDtypeStruct((3, SLOTS, 3 * Q), BF16),
        ),
        in_specs=[VM] * 4 + [hbm] * 5,
        out_specs=(VM, VM),
        scratch_shapes=[
            pltpu.VMEM((NDP * Q, D), BF16),
            pltpu.VMEM((NDP * Q, D), BF16),
            pltpu.VMEM((NDP * Q, D), BF16),
            pltpu.VMEM((SLOTS, D), F32),
            pltpu.VMEM((SLOTS, D), F32),
            pltpu.SemaphoreType.DMA((16,)),
        ],
        compiler_params=params(),
        cost_estimate=cost(1e6, 1e5),
    )(x, d, hid, perm, own, from_left, from_right, f_low, f_up)
    go_low, go_up, gl_low, gl_up, gr_low, gr_up = pl.pallas_call(
        grad_kernel,
        out_shape=(half,) * 6,
        in_specs=[VM] * 3,
        out_specs=(VM,) * 6,
        compiler_params=params(),
        cost_estimate=cost(1e6, 1e5),
    )(x, d, mine)

    def plus(a, *b):
        return (a.astype(F32) + jnp.concatenate(b, axis=0).astype(F32)).astype(BF16)

    a_up = lax.ppermute(gr_up, "dp", right)
    b_low = lax.ppermute(gl_low, "dp", left)
    a_low = lax.ppermute(plus(gr_low, came_gate, came_u), "dp", right)
    b_up = lax.ppermute(plus(gl_up, came_v, came_down), "dp", left)
    back = lax.optimization_barrier((back, came_gate, came_down))[0]
    returned = lax.all_to_all(
        back.reshape(OWN, CH * CAP, 256), "expert", split_axis=0, concat_axis=0, tiled=True
    ).reshape(OWN * CH * CAP, 256)

    hot_z = lax.psum_scatter(hot_y, "expert", scatter_dimension=0, axis_index_groups=along_z, tiled=True)
    hot_low = hot_z[0:32].T
    hot_up_part = jnp.concatenate([hot_z[32:, :Q], hot_z[32:, Q:]], axis=0).T

    mixed, token_grad, route_grad = pl.pallas_call(
        combine_kernel,
        out_shape=(
            jax.ShapeDtypeStruct((T, D), BF16),
            jax.ShapeDtypeStruct((T, D), BF16),
            jax.ShapeDtypeStruct((2, T), F32),
        ),
        in_specs=[VM] * 9,
        out_specs=(VM, VM, VM),
        scratch_shapes=[pltpu.VMEM((SLOTS + HOT, D), F32), pltpu.VMEM((SLOTS + HOT, D), F32)],
        compiler_params=params(),
        cost_estimate=cost(4e9, 6e6),
    )(returned, hot_own, back_r, back_l, back_f, cotangent, ids_t, gain_t, perm_t)
    third = jax.ShapeDtypeStruct((1, Q, D), BF16)
    gate_grad, up_grad, down_grad = pl.pallas_call(
        finish_kernel,
        out_shape=(third,) * 3,
        grid=(4,),
        in_specs=[pl.BlockSpec((HALF, D // 4), lambda i: (0, i))] * 6,
        out_specs=(pl.BlockSpec((1, Q, D // 4), lambda i: (0, 0, i)),) * 3,
        compiler_params=params(),
        cost_estimate=cost(1e6, 10e6),
    )(go_low, go_up, a_low, a_up, b_low, b_up)
    return (
        mixed,
        token_grad,
        route_grad.T,
        gate_grad,
        up_grad,
        down_grad,
        hot_low[None, 0:Q],
        hot_low[None, Q:],
        hot_up_part[None],
    )


def solution(mesh):
    rows = P(("expert", "dp"), None)
    cold = P("expert", "dp", None)
    hot = P(None, "dp", None)
    split = P(None, "dp", "expert")
    return jax.shard_map(
        local,
        mesh=mesh,
        in_specs=(rows, rows, rows, rows, cold, cold, cold, hot, hot, hot),
        out_specs=(rows, rows, rows, cold, cold, cold, split, split, split),
        check_vma=False,
    )
```

```python
import jax
import jax.numpy as jnp
import numpy as np
from jax import lax
from jax.experimental import pallas as pl
from jax.experimental.pallas import tpu as pltpu
from jax.sharding import PartitionSpec as P

F32 = jnp.float32
BF16 = jnp.bfloat16
T = 128
D = 2048
Q = 192
OWN = 64
CAP = 5
SLOTS = OWN * CAP
HOT = 32
NDP = 4
HALF = 3 * Q // 2
CH = 16
PEERS = 8
GROUP = PEERS * CAP
BLOCK = PEERS * CH * CAP
VMEM = 56 * 1024 * 1024


def packing():
    out = np.zeros((BLOCK, BLOCK), np.float32)
    for p in range(PEERS):
        for c in range(CH):
            for s in range(CAP):
                out[p * CH * CAP + c * CAP + s, c * GROUP + p * CAP + s] = 1.0
    return out


def dot(a, b, ca, cb):
    return lax.dot_general(a, b, (((ca,), (cb,)), ((), ())), preferred_element_type=F32)


def diagonal(n):
    return lax.broadcasted_iota(jnp.int32, (n, n), 0) == lax.broadcasted_iota(jnp.int32, (n, n), 1)


def as_row(col):
    return jnp.sum(jnp.where(diagonal(col.shape[0]), col, 0.0), axis=0, keepdims=True)


def as_col(row):
    return jnp.sum(jnp.where(diagonal(row.shape[1]), row, 0.0), axis=1, keepdims=True)


def pair_ids(ids):
    r0, r1 = ids[0:1, :].astype(F32), ids[1:2, :].astype(F32)
    col = jnp.concatenate([as_col(r0), as_col(r1)], axis=0)
    row = jnp.concatenate([r0, r1], axis=1)
    first = lax.broadcasted_iota(jnp.int32, (2 * T, 2 * T), 0)
    second = lax.broadcasted_iota(jnp.int32, (2 * T, 2 * T), 1)
    return col, row, first, second


def slot_of(ident, rank):
    return jnp.where(ident < float(OWN), ident * float(CAP) + rank, float(SLOTS) + rank)


def pack(perm, left, right, out):
    def body(g, carry):
        r0 = pl.multiple_of(g * GROUP, 8)
        pieces = []
        for c in range(CH):
            pieces.append(
                jnp.concatenate(
                    [
                        left[pl.ds(r0, GROUP), c * 128 : (c + 1) * 128],
                        right[pl.ds(r0, GROUP), c * 128 : (c + 1) * 128],
                    ],
                    axis=1,
                )
            )
        rows = jnp.concatenate(pieces, axis=0).astype(BF16)
        out[pl.ds(pl.multiple_of(g * BLOCK, 128), BLOCK), :] = dot(perm[...], rows, 1, 0).astype(BF16)
        return carry

    lax.fori_loop(0, OWN // PEERS, body, 0, unroll=True)


def unpack(perm, src, left, right):
    def body(g, carry):
        r0 = pl.multiple_of(g * GROUP, 8)
        rows = dot(perm[...], src[pl.ds(pl.multiple_of(g * BLOCK, 128), BLOCK), :], 1, 0)
        for c in range(CH):
            left[pl.ds(r0, GROUP), c * 128 : (c + 1) * 128] = rows[c * GROUP : (c + 1) * GROUP, :128]
            right[pl.ds(r0, GROUP), c * 128 : (c + 1) * 128] = rows[c * GROUP : (c + 1) * GROUP, 128:]
        return carry

    lax.fori_loop(0, OWN // PEERS, body, 0, unroll=True)


def dispatch_kernel(tok, cot, ids, gain, perm, send, hot, rx, rd):
    col, row, first, second = pair_ids(ids[...])
    rank = jnp.sum(jnp.where((col == row) & (first < second), 1.0, 0.0), axis=0, keepdims=True)
    target = slot_of(row, rank)
    slot = lax.broadcasted_iota(jnp.int32, (SLOTS + HOT, 2 * T), 0).astype(F32)
    place = jnp.where(slot == target, 1.0, 0.0)
    g = gain[...]
    g_row = jnp.concatenate([g[0:1, :], g[1:2, :]], axis=1)
    g_slot = jnp.sum(place * g_row, axis=1, keepdims=True)
    of_tok = (place[:, :T] + place[:, T:]).astype(BF16)
    for c in range(4):
        cols = slice(c * 512, (c + 1) * 512)
        rx[:, cols] = dot(of_tok, tok[:, cols], 1, 0)
        rd[:, cols] = dot(of_tok, cot[:, cols], 1, 0) * g_slot
    hot[0:HOT, :] = rx[SLOTS:, :].astype(BF16)
    hot[HOT:, :] = rd[SLOTS:, :].astype(BF16)
    pack(perm, rx, rd, send)


def expert_math(x, d, wg, wu, wd):
    return hidden(dot(x, wg, 1, 1), dot(x, wu, 1, 1), dot(d, wd, 1, 1))


def hidden(pre_g, pre_u, d_act):
    sig = 1.0 / (1.0 + jnp.exp(-pre_g))
    silu = pre_g * sig
    act = (silu * pre_u).astype(BF16)
    d_g = (d_act * pre_u * (sig * (1.0 + pre_g * (1.0 - sig)))).astype(BF16)
    d_u = (d_act * silu).astype(BF16)
    return act, d_g, d_u


def hot_kernel(place, rows, other, wg, wu, wd, p0, p1, p2, p3, keep):
    starts = [pl.multiple_of(lax.rem(place[1] + i, NDP) * 2 * HOT, 2 * HOT) for i in (0, 3, 1, 2)]
    pairs = [(src, s) for src in (rows, other) for s in starts]
    x = jnp.concatenate([src[pl.ds(s, HOT), :] for src, s in pairs], axis=0)
    d = jnp.concatenate([src[pl.ds(s + HOT, HOT), :] for src, s in pairs], axis=0)
    act, d_g, d_u = expert_math(x, d, wg[0], wu[0], wd[0])
    n = NDP * HOT
    for c in range(4):
        cols = slice(c * 512, (c + 1) * 512)
        out = dot(act[:n], wd[0, :, cols], 1, 0).astype(BF16)
        dx = (dot(d_g[:n], wg[0, :, cols], 1, 0) + dot(d_u[:n], wu[0, :, cols], 1, 0)).astype(BF16)
        for r, part in enumerate((p0, p1, p2, p3)):
            part[0:HOT, cols] = out[r * HOT : (r + 1) * HOT]
            part[HOT:, cols] = dx[r * HOT : (r + 1) * HOT]
    mine = place[0] == 0
    both = jnp.concatenate([d_g, d_u], axis=1)
    for c in range(8):
        cols = slice(c * 256, (c + 1) * 256)
        gu = dot(x[:, cols], both, 0, 0).reshape(4, 2, 32, 2 * Q)
        dn = dot(d[:, cols], act, 0, 0).reshape(4, 2, 32, Q)
        for i in range(4):
            base = (c * 4 + i) * 48
            keep[base : base + 32, :] = jnp.where(mine, gu[i, 0], gu[i, 1])
            pick = jnp.where(mine, dn[i, 0], dn[i, 1])
            keep[base + 32 : base + 48, :] = jnp.concatenate([pick[:16], pick[16:]], axis=1)


def fill(parts, wg, wu, wd, at, sems, i):
    low, up = parts
    return [
        pltpu.make_async_copy(low.at[0:Q, :], wg.at[at : at + Q, :], sems.at[i]),
        pltpu.make_async_copy(low.at[Q:HALF, :], wu.at[at : at + Q // 2, :], sems.at[i + 1]),
        pltpu.make_async_copy(up.at[0 : Q // 2, :], wu.at[at + Q // 2 : at + Q, :], sems.at[i + 2]),
        pltpu.make_async_copy(up.at[Q // 2 : HALF, :], wd.at[at : at + Q, :], sems.at[i + 3]),
    ]


def far_kernel(rows, perm, low, up, x_out, d_out, hid, g_gate, g_u, g_v, g_down, xf, df):
    unpack(perm, rows, xf, df)
    x_out[...] = xf[...].astype(BF16)
    d_out[...] = df[...].astype(BF16)
    wu = jnp.concatenate([low[Q:HALF, :], up[0 : Q // 2, :]], axis=0)
    act, d_g, d_u = expert_math(x_out[...], d_out[...], low[0:Q, :], wu, up[Q // 2 : HALF, :])
    hid[0, :, :] = act
    hid[1, :, :] = d_g
    hid[2, :, :] = d_u
    both = jnp.concatenate([d_g, d_u], axis=1)
    for c in range(4):
        cols = slice(c * 512, (c + 1) * 512)
        gu = dot(both, x_out[:, cols], 0, 0).astype(BF16)
        g_down[:, cols] = dot(act, d_out[:, cols], 0, 0).astype(BF16)
        g_gate[:, cols] = gu[0:Q]
        g_u[:, cols] = gu[Q:HALF]
        g_v[:, cols] = gu[HALF:]


def near_kernel(x, d, hid, perm, *refs):
    whole, far, (back, mine, wg, wu, wd, of, df, sems) = refs[:3], refs[3:5], refs[5:]
    copies = []
    for i, src in enumerate(whole):
        copies += fill((src.at[0:HALF, :], src.at[HALF : 3 * Q, :]), wg, wu, wd, i * Q, sems, 4 * i)
    copies += fill(far, wg, wu, wd, 3 * Q, sems, 12)
    for k in range(4):
        for i in range(0, 16, 4):
            copies[i + k].start()
    n = 3 * Q
    for i in range(0, 16, 4):
        copies[i].wait()
    pre_g = dot(x[...], wg[0:n, :], 1, 1)
    for i in range(0, 16, 4):
        copies[i + 1].wait()
        copies[i + 2].wait()
    pre_u = dot(x[...], wu[0:n, :], 1, 1)
    for i in range(0, 16, 4):
        copies[i + 3].wait()
    d_act = dot(d[...], wd[0:n, :], 1, 1)
    act, d_g, d_u = hidden(pre_g, pre_u, d_act)
    mine[0, :, :] = act
    mine[1, :, :] = d_g
    mine[2, :, :] = d_u
    act = jnp.concatenate([act, hid[0]], axis=1)
    d_g = jnp.concatenate([d_g, hid[1]], axis=1)
    d_u = jnp.concatenate([d_u, hid[2]], axis=1)
    for c in range(4):
        cols = slice(c * 512, (c + 1) * 512)
        of[:, cols] = dot(act, wd[:, cols], 1, 0)
        df[:, cols] = dot(d_g, wg[:, cols], 1, 0) + dot(d_u, wu[:, cols], 1, 0)
    pack(perm, of, df, back)


def grad_kernel(x, d, mine, *outs):
    for s in range(3):
        low, up = outs[2 * s], outs[2 * s + 1]
        at = slice(s * Q, (s + 1) * Q)
        act = mine[0, :, at]
        both = jnp.concatenate([mine[1, :, at], mine[2, :, at]], axis=1)
        for c in range(4):
            cols = slice(c * 512, (c + 1) * 512)
            gu = dot(both, x[:, cols], 0, 0).astype(BF16)
            low[:, cols] = gu[0:HALF]
            up[0 : Q // 2, cols] = gu[HALF:]
            up[Q // 2 :, cols] = dot(act, d[:, cols], 0, 0).astype(BF16)


def finish_kernel(a_low, a_up, b_low, b_up, c_low, c_up, gate, up, down):
    low = (a_low[...].astype(F32) + b_low[...].astype(F32) + c_low[...].astype(F32)).astype(BF16)
    top = (a_up[...].astype(F32) + b_up[...].astype(F32) + c_up[...].astype(F32)).astype(BF16)
    gate[0] = low[0:Q]
    up[0, 0 : Q // 2, :] = low[Q:]
    up[0, Q // 2 :, :] = top[0 : Q // 2]
    down[0] = top[Q // 2 :]


def combine_kernel(back, h0, h1, h2, h3, cot, ids, gain, perm, mixed, tgrad, rgrad, of, df):
    unpack(perm, back, of, df)
    hot = h0[...].astype(F32) + h1[...].astype(F32) + h2[...].astype(F32) + h3[...].astype(F32)
    of[SLOTS:, :] = hot[0:HOT, :]
    df[SLOTS:, :] = hot[HOT:, :]
    col, row, first, second = pair_ids(ids[...])
    rank = jnp.sum(jnp.where((col == row) & (second < first), 1.0, 0.0), axis=1, keepdims=True)
    target = slot_of(col, rank)
    slot = lax.broadcasted_iota(jnp.int32, (2 * T, SLOTS + HOT), 1).astype(F32)
    place = jnp.where(slot == target, 1.0, 0.0)
    p0, p1 = place[:T].astype(BF16), place[T:].astype(BF16)
    both = (place[:T] + place[T:]).astype(BF16)
    g0, g1 = as_col(gain[0:1, :]), as_col(gain[1:2, :])
    r0 = jnp.zeros((T, 1), F32)
    r1 = jnp.zeros((T, 1), F32)
    for c in range(4):
        cols = slice(c * 512, (c + 1) * 512)
        o = of[:, cols].astype(BF16)
        e0, e1 = dot(p0, o, 1, 0), dot(p1, o, 1, 0)
        ct = cot[:, cols].astype(F32)
        mixed[:, cols] = (g0 * e0 + g1 * e1).astype(BF16)
        r0 = r0 + jnp.sum(ct * e0, axis=1, keepdims=True)
        r1 = r1 + jnp.sum(ct * e1, axis=1, keepdims=True)
        tgrad[:, cols] = dot(both, df[:, cols].astype(BF16), 1, 0).astype(BF16)
    rgrad[0:1, :] = as_row(r0)
    rgrad[1:2, :] = as_row(r1)


def params(**kw):
    return pltpu.CompilerParams(vmem_limit_bytes=VMEM, **kw)


def cost(flops, nbytes):
    return pl.CostEstimate(flops=int(flops), bytes_accessed=int(nbytes), transcendentals=0)


VM = pl.BlockSpec(memory_space=pltpu.VMEM)


def local(tokens, cotangent, route_ids, route_weights, cold_gate, cold_up, cold_down, hot_gate, hot_up, hot_down):
    perm = jnp.asarray(packing(), BF16)
    perm_t = jnp.asarray(packing().T, BF16)
    ids_t, gain_t = route_ids.T, route_weights.T
    expert = lax.axis_index("expert")
    place = jnp.stack([lax.rem(expert, 2), lax.axis_index("dp")])

    right = [(i, (i + 1) % NDP) for i in range(NDP)]
    left = [(i, (i - 1) % NDP) for i in range(NDP)]
    own = jnp.concatenate([cold_gate[0], cold_up[0], cold_down[0]], axis=0)
    from_left = lax.ppermute(own, "dp", right)
    from_right = lax.ppermute(own, "dp", left)
    f_low = lax.ppermute(from_left[:HALF], "dp", right)
    f_up = lax.ppermute(from_right[HALF:], "dp", left)
    tokens, _ = lax.optimization_barrier((tokens, own))

    send, hot_rows = pl.pallas_call(
        dispatch_kernel,
        out_shape=(
            jax.ShapeDtypeStruct((OWN * CH * CAP, 256), BF16),
            jax.ShapeDtypeStruct((2 * HOT, D), BF16),
        ),
        in_specs=[VM] * 5,
        out_specs=(VM, VM),
        scratch_shapes=[pltpu.VMEM((SLOTS + HOT, D), F32), pltpu.VMEM((SLOTS + HOT, D), F32)],
        compiler_params=params(),
        cost_estimate=cost(4e9, 6e6),
    )(tokens, cotangent, ids_t, gain_t, perm)

    far = [(i, (i + 2) % NDP) for i in range(NDP)]
    hot_all = lax.all_gather(hot_rows, "dp", axis=0, tiled=True)
    arrived = lax.all_to_all(
        send.reshape(OWN, CH * CAP, 256), "expert", split_axis=0, concat_axis=0, tiled=True
    ).reshape(OWN * CH * CAP, 256)

    hot_all = lax.optimization_barrier((hot_all, from_left, from_right))[0]
    hot_other = lax.ppermute(hot_all, "expert", [(i, i ^ 1) for i in range(OWN)])
    hot_own, to_l, to_r, to_f, keep = pl.pallas_call(
        hot_kernel,
        out_shape=(
            jax.ShapeDtypeStruct((2 * HOT, D), BF16),
            jax.ShapeDtypeStruct((2 * HOT, D), BF16),
            jax.ShapeDtypeStruct((2 * HOT, D), BF16),
            jax.ShapeDtypeStruct((2 * HOT, D), BF16),
            jax.ShapeDtypeStruct((OWN // 2 * 48, 2 * Q), F32),
        ),
        in_specs=[pl.BlockSpec(memory_space=pltpu.SMEM)] + [VM] * 5,
        out_specs=(VM,) * 5,
        compiler_params=params(),
        cost_estimate=cost(3e10, 9e6),
    )(place, hot_all, hot_other, hot_gate, hot_up, hot_down)
    back_r = lax.ppermute(to_l, "dp", left)
    back_l = lax.ppermute(to_r, "dp", right)
    back_f = lax.ppermute(to_f, "dp", far)
    keep = lax.optimization_barrier((keep, f_low, f_up))[0]
    along_y = [[y * 16 + r for y in range(4)] for r in range(16)]
    along_z = [[y * 16 + z * 2 + c for z in range(8)] for y in range(4) for c in range(2)]
    hot_y = lax.psum_scatter(keep, "expert", scatter_dimension=0, axis_index_groups=along_y, tiled=True)
    half = jax.ShapeDtypeStruct((HALF, D), BF16)
    x, d, hid, gf_gate, gf_u, gf_v, gf_down = pl.pallas_call(
        far_kernel,
        out_shape=(
            jax.ShapeDtypeStruct((SLOTS, D), BF16),
            jax.ShapeDtypeStruct((SLOTS, D), BF16),
            jax.ShapeDtypeStruct((3, SLOTS, Q), BF16),
            jax.ShapeDtypeStruct((Q, D), BF16),
            jax.ShapeDtypeStruct((Q // 2, D), BF16),
            jax.ShapeDtypeStruct((Q // 2, D), BF16),
            jax.ShapeDtypeStruct((Q, D), BF16),
        ),
        in_specs=[VM] * 4,
        out_specs=(VM,) * 7,
        scratch_shapes=[pltpu.VMEM((SLOTS, D), F32), pltpu.VMEM((SLOTS, D), F32)],
        compiler_params=params(),
        cost_estimate=cost(4e9, 12e6),
    )(arrived, perm_t, f_low, f_up)
    came_gate = lax.ppermute(gf_gate, "dp", right)
    came_down = lax.ppermute(gf_down, "dp", left)
    gf_u, hot_y = lax.optimization_barrier((gf_u, hot_y))
    came_u = lax.ppermute(gf_u, "dp", right)
    came_v = lax.ppermute(gf_v, "dp", left)
    hbm = pl.BlockSpec(memory_space=pl.ANY)
    back, mine = pl.pallas_call(
        near_kernel,
        out_shape=(
            jax.ShapeDtypeStruct((OWN * CH * CAP, 256), BF16),
            jax.ShapeDtypeStruct((3, SLOTS, 3 * Q), BF16),
        ),
        in_specs=[VM] * 4 + [hbm] * 5,
        out_specs=(VM, VM),
        scratch_shapes=[
            pltpu.VMEM((NDP * Q, D), BF16),
            pltpu.VMEM((NDP * Q, D), BF16),
            pltpu.VMEM((NDP * Q, D), BF16),
            pltpu.VMEM((SLOTS, D), F32),
            pltpu.VMEM((SLOTS, D), F32),
            pltpu.SemaphoreType.DMA((16,)),
        ],
        compiler_params=params(),
        cost_estimate=cost(1e6, 1e5),
    )(x, d, hid, perm, own, from_left, from_right, f_low, f_up)
    go_low, go_up, gl_low, gl_up, gr_low, gr_up = pl.pallas_call(
        grad_kernel,
        out_shape=(half,) * 6,
        in_specs=[VM] * 3,
        out_specs=(VM,) * 6,
        compiler_params=params(),
        cost_estimate=cost(1e6, 1e5),
    )(x, d, mine)

    def plus(a, *b):
        return (a.astype(F32) + jnp.concatenate(b, axis=0).astype(F32)).astype(BF16)

    a_up = lax.ppermute(gr_up, "dp", right)
    b_low = lax.ppermute(gl_low, "dp", left)
    a_low = lax.ppermute(plus(gr_low, came_gate, came_u), "dp", right)
    b_up = lax.ppermute(plus(gl_up, came_v, came_down), "dp", left)
    back = lax.optimization_barrier((back, came_gate, came_down))[0]
    returned = lax.all_to_all(
        back.reshape(OWN, CH * CAP, 256), "expert", split_axis=0, concat_axis=0, tiled=True
    ).reshape(OWN * CH * CAP, 256)

    hot_z = lax.psum_scatter(hot_y, "expert", scatter_dimension=0, axis_index_groups=along_z, tiled=True)
    hot_low = hot_z[0:32].T
    hot_up_part = jnp.concatenate([hot_z[32:, :Q], hot_z[32:, Q:]], axis=0).T

    mixed, token_grad, route_grad = pl.pallas_call(
        combine_kernel,
        out_shape=(
            jax.ShapeDtypeStruct((T, D), BF16),
            jax.ShapeDtypeStruct((T, D), BF16),
            jax.ShapeDtypeStruct((2, T), F32),
        ),
        in_specs=[VM] * 9,
        out_specs=(VM, VM, VM),
        scratch_shapes=[pltpu.VMEM((SLOTS + HOT, D), F32), pltpu.VMEM((SLOTS + HOT, D), F32)],
        compiler_params=params(),
        cost_estimate=cost(4e9, 6e6),
    )(returned, hot_own, back_r, back_l, back_f, cotangent, ids_t, gain_t, perm_t)
    third = jax.ShapeDtypeStruct((1, Q, D), BF16)
    gate_grad, up_grad, down_grad = pl.pallas_call(
        finish_kernel,
        out_shape=(third,) * 3,
        grid=(4,),
        in_specs=[pl.BlockSpec((HALF, D // 4), lambda i: (0, i))] * 6,
        out_specs=(pl.BlockSpec((1, Q, D // 4), lambda i: (0, 0, i)),) * 3,
        compiler_params=params(),
        cost_estimate=cost(1e6, 10e6),
    )(go_low, go_up, a_low, a_up, b_low, b_up)
    return (
        mixed,
        token_grad,
        route_grad.T,
        gate_grad,
        up_grad,
        down_grad,
        hot_low[None, 0:Q],
        hot_low[None, Q:],
        hot_up_part[None],
    )


def solution(mesh):
    rows = P(("expert", "dp"), None)
    cold = P("expert", "dp", None)
    hot = P(None, "dp", None)
    split = P(None, "dp", "expert")
    return jax.shard_map(
        local,
        mesh=mesh,
        in_specs=(rows, rows, rows, rows, cold, cold, cold, hot, hot, hot),
        out_specs=(rows, rows, rows, cold, cold, cold, split, split, split),
        check_vma=False,
    )
```

```python
import functools

import jax
import jax.numpy as jnp
import numpy as np
from jax import lax
from jax.experimental import pallas as pl
from jax.experimental.pallas import tpu as pltpu
from jax.sharding import PartitionSpec as P

F32 = jnp.float32
BF16 = jnp.bfloat16
T = 128
D = 2048
Q = 192
OWN = 64
CAP = 5
SLOTS = OWN * CAP
HOT = 32
NDP = 4
HALF = 3 * Q // 2
CH = 16
PEERS = 8
GROUP = PEERS * CAP
BLOCK = PEERS * CH * CAP
VMEM = 56 * 1024 * 1024


def packing():
    out = np.zeros((BLOCK, BLOCK), np.float32)
    for p in range(PEERS):
        for c in range(CH):
            for s in range(CAP):
                out[p * CH * CAP + c * CAP + s, c * GROUP + p * CAP + s] = 1.0
    return out


def dot(a, b, ca, cb):
    return lax.dot_general(a, b, (((ca,), (cb,)), ((), ())), preferred_element_type=F32)


def diagonal(n):
    return lax.broadcasted_iota(jnp.int32, (n, n), 0) == lax.broadcasted_iota(jnp.int32, (n, n), 1)


def as_row(col):
    return jnp.sum(jnp.where(diagonal(col.shape[0]), col, 0.0), axis=0, keepdims=True)


def as_col(row):
    return jnp.sum(jnp.where(diagonal(row.shape[1]), row, 0.0), axis=1, keepdims=True)


def pair_ids(ids):
    r0, r1 = ids[0:1, :].astype(F32), ids[1:2, :].astype(F32)
    col = jnp.concatenate([as_col(r0), as_col(r1)], axis=0)
    row = jnp.concatenate([r0, r1], axis=1)
    first = lax.broadcasted_iota(jnp.int32, (2 * T, 2 * T), 0)
    second = lax.broadcasted_iota(jnp.int32, (2 * T, 2 * T), 1)
    return col, row, first, second


def slot_of(ident, rank):
    return jnp.where(ident < float(OWN), ident * float(CAP) + rank, float(SLOTS) + rank)


def pack(perm, left, right, out):
    def body(g, carry):
        r0 = pl.multiple_of(g * GROUP, 8)
        pieces = []
        for c in range(CH):
            pieces.append(
                jnp.concatenate(
                    [
                        left[pl.ds(r0, GROUP), c * 128 : (c + 1) * 128],
                        right[pl.ds(r0, GROUP), c * 128 : (c + 1) * 128],
                    ],
                    axis=1,
                )
            )
        rows = jnp.concatenate(pieces, axis=0).astype(BF16)
        out[pl.ds(pl.multiple_of(g * BLOCK, 128), BLOCK), :] = dot(perm[...], rows, 1, 0).astype(BF16)
        return carry

    lax.fori_loop(0, OWN // PEERS, body, 0, unroll=True)


def unpack(perm, src, left, right):
    def body(g, carry):
        r0 = pl.multiple_of(g * GROUP, 8)
        rows = dot(perm[...], src[pl.ds(pl.multiple_of(g * BLOCK, 128), BLOCK), :], 1, 0)
        for c in range(CH):
            left[pl.ds(r0, GROUP), c * 128 : (c + 1) * 128] = rows[c * GROUP : (c + 1) * GROUP, :128]
            right[pl.ds(r0, GROUP), c * 128 : (c + 1) * 128] = rows[c * GROUP : (c + 1) * GROUP, 128:]
        return carry

    lax.fori_loop(0, OWN // PEERS, body, 0, unroll=True)


def dispatch_kernel(tok, cot, ids, gain, perm, send, hot, rx, rd):
    col, row, first, second = pair_ids(ids[...])
    rank = jnp.sum(jnp.where((col == row) & (first < second), 1.0, 0.0), axis=0, keepdims=True)
    target = slot_of(row, rank)
    slot = lax.broadcasted_iota(jnp.int32, (SLOTS + HOT, 2 * T), 0).astype(F32)
    place = jnp.where(slot == target, 1.0, 0.0)
    g = gain[...]
    g_row = jnp.concatenate([g[0:1, :], g[1:2, :]], axis=1)
    g_slot = jnp.sum(place * g_row, axis=1, keepdims=True)
    of_tok = (place[:, :T] + place[:, T:]).astype(BF16)
    for c in range(4):
        cols = slice(c * 512, (c + 1) * 512)
        rx[:, cols] = dot(of_tok, tok[:, cols], 1, 0)
        rd[:, cols] = dot(of_tok, cot[:, cols], 1, 0) * g_slot
    hot[0:HOT, :] = rx[SLOTS:, :].astype(BF16)
    hot[HOT:, :] = rd[SLOTS:, :].astype(BF16)
    pack(perm, rx, rd, send)


def expert_math(x, d, wg, wu, wd):
    return hidden(dot(x, wg, 1, 1), dot(x, wu, 1, 1), dot(d, wd, 1, 1))


def hidden(pre_g, pre_u, d_act):
    sig = 1.0 / (1.0 + jnp.exp(-pre_g))
    silu = pre_g * sig
    act = (silu * pre_u).astype(BF16)
    d_g = (d_act * pre_u * (sig * (1.0 + pre_g * (1.0 - sig)))).astype(BF16)
    d_u = (d_act * silu).astype(BF16)
    return act, d_g, d_u


def hot_kernel(place, rows, other, wg, wu, wd, p0, p1, p2, p3, keep):
    starts = [pl.multiple_of(lax.rem(place[1] + i, NDP) * 2 * HOT, 2 * HOT) for i in (0, 3, 1, 2)]
    pairs = [(src, s) for src in (rows, other) for s in starts]
    x = jnp.concatenate([src[pl.ds(s, HOT), :] for src, s in pairs], axis=0)
    d = jnp.concatenate([src[pl.ds(s + HOT, HOT), :] for src, s in pairs], axis=0)
    act, d_g, d_u = expert_math(x, d, wg[0], wu[0], wd[0])
    n = NDP * HOT
    for c in range(4):
        cols = slice(c * 512, (c + 1) * 512)
        out = dot(act[:n], wd[0, :, cols], 1, 0).astype(BF16)
        dx = (dot(d_g[:n], wg[0, :, cols], 1, 0) + dot(d_u[:n], wu[0, :, cols], 1, 0)).astype(BF16)
        for r, part in enumerate((p0, p1, p2, p3)):
            part[0:HOT, cols] = out[r * HOT : (r + 1) * HOT]
            part[HOT:, cols] = dx[r * HOT : (r + 1) * HOT]
    mine = place[0] == 0
    both = jnp.concatenate([d_g, d_u], axis=1)
    for c in range(8):
        cols = slice(c * 256, (c + 1) * 256)
        gu = dot(x[:, cols], both, 0, 0).reshape(4, 2, 32, 2 * Q)
        dn = dot(d[:, cols], act, 0, 0).reshape(4, 2, 32, Q)
        for i in range(4):
            base = (c * 4 + i) * 48
            keep[base : base + 32, :] = jnp.where(mine, gu[i, 0], gu[i, 1])
            pick = jnp.where(mine, dn[i, 0], dn[i, 1])
            keep[base + 32 : base + 48, :] = jnp.concatenate([pick[:16], pick[16:]], axis=1)


def fill(parts, wg, wu, wd, at, sems, i):
    low, up = parts
    return [
        pltpu.make_async_copy(low.at[0:Q, :], wg.at[at : at + Q, :], sems.at[i]),
        pltpu.make_async_copy(low.at[Q:HALF, :], wu.at[at : at + Q // 2, :], sems.at[i + 1]),
        pltpu.make_async_copy(up.at[0 : Q // 2, :], wu.at[at + Q // 2 : at + Q, :], sems.at[i + 2]),
        pltpu.make_async_copy(up.at[Q // 2 : HALF, :], wd.at[at : at + Q, :], sems.at[i + 3]),
    ]


def far_kernel(rows, perm, low, up, x_out, d_out, hid, g_gate, g_u, g_v, g_down, xf, df):
    unpack(perm, rows, xf, df)
    x_out[...] = xf[...].astype(BF16)
    d_out[...] = df[...].astype(BF16)
    wu = jnp.concatenate([low[Q:HALF, :], up[0 : Q // 2, :]], axis=0)
    act, d_g, d_u = expert_math(x_out[...], d_out[...], low[0:Q, :], wu, up[Q // 2 : HALF, :])
    hid[0, :, :] = act
    hid[1, :, :] = d_g
    hid[2, :, :] = d_u
    both = jnp.concatenate([d_g, d_u], axis=1)
    for c in range(4):
        cols = slice(c * 512, (c + 1) * 512)
        gu = dot(both, x_out[:, cols], 0, 0).astype(BF16)
        g_down[:, cols] = dot(act, d_out[:, cols], 0, 0).astype(BF16)
        g_gate[:, cols] = gu[0:Q]
        g_u[:, cols] = gu[Q:HALF]
        g_v[:, cols] = gu[HALF:]


def near_kernel(x, d, hid, perm, *refs):
    whole, far, (back, mine, wg, wu, wd, of, df, sems) = refs[:3], refs[3:5], refs[5:]
    copies = []
    for i, src in enumerate(whole):
        copies += fill((src.at[0:HALF, :], src.at[HALF : 3 * Q, :]), wg, wu, wd, i * Q, sems, 4 * i)
    copies += fill(far, wg, wu, wd, 3 * Q, sems, 12)
    for k in range(4):
        for i in range(0, 16, 4):
            copies[i + k].start()
    n = 3 * Q
    for i in range(0, 16, 4):
        copies[i].wait()
    pre_g = dot(x[...], wg[0:n, :], 1, 1)
    for i in range(0, 16, 4):
        copies[i + 1].wait()
        copies[i + 2].wait()
    pre_u = dot(x[...], wu[0:n, :], 1, 1)
    for i in range(0, 16, 4):
        copies[i + 3].wait()
    d_act = dot(d[...], wd[0:n, :], 1, 1)
    act, d_g, d_u = hidden(pre_g, pre_u, d_act)
    mine[0, :, :] = act
    mine[1, :, :] = d_g
    mine[2, :, :] = d_u
    act = jnp.concatenate([act, hid[0]], axis=1)
    d_g = jnp.concatenate([d_g, hid[1]], axis=1)
    d_u = jnp.concatenate([d_u, hid[2]], axis=1)
    for c in range(4):
        cols = slice(c * 512, (c + 1) * 512)
        of[:, cols] = dot(act, wd[:, cols], 1, 0)
        df[:, cols] = dot(d_g, wg[:, cols], 1, 0) + dot(d_u, wu[:, cols], 1, 0)
    pack(perm, of, df, back)


def grad_kernel(shards, x, d, mine, *outs):
    for i, s in enumerate(shards):
        low, up = outs[2 * i], outs[2 * i + 1]
        at = slice(s * Q, (s + 1) * Q)
        act = mine[0, :, at]
        both = jnp.concatenate([mine[1, :, at], mine[2, :, at]], axis=1)
        for c in range(4):
            cols = slice(c * 512, (c + 1) * 512)
            gu = dot(both, x[:, cols], 0, 0).astype(BF16)
            low[:, cols] = gu[0:HALF]
            up[0 : Q // 2, cols] = gu[HALF:]
            up[Q // 2 :, cols] = dot(act, d[:, cols], 0, 0).astype(BF16)


def finish_kernel(a_low, a_up, b_low, b_up, c_low, c_up, gate, up, down):
    low = (a_low[...].astype(F32) + b_low[...].astype(F32) + c_low[...].astype(F32)).astype(BF16)
    top = (a_up[...].astype(F32) + b_up[...].astype(F32) + c_up[...].astype(F32)).astype(BF16)
    gate[0] = low[0:Q]
    up[0, 0 : Q // 2, :] = low[Q:]
    up[0, Q // 2 :, :] = top[0 : Q // 2]
    down[0] = top[Q // 2 :]


def combine_kernel(back, h0, h1, h2, h3, cot, ids, gain, perm, mixed, tgrad, rgrad, of, df):
    unpack(perm, back, of, df)
    hot = h0[...].astype(F32) + h1[...].astype(F32) + h2[...].astype(F32) + h3[...].astype(F32)
    of[SLOTS:, :] = hot[0:HOT, :]
    df[SLOTS:, :] = hot[HOT:, :]
    col, row, first, second = pair_ids(ids[...])
    rank = jnp.sum(jnp.where((col == row) & (second < first), 1.0, 0.0), axis=1, keepdims=True)
    target = slot_of(col, rank)
    slot = lax.broadcasted_iota(jnp.int32, (2 * T, SLOTS + HOT), 1).astype(F32)
    place = jnp.where(slot == target, 1.0, 0.0)
    p0, p1 = place[:T].astype(BF16), place[T:].astype(BF16)
    both = (place[:T] + place[T:]).astype(BF16)
    g0, g1 = as_col(gain[0:1, :]), as_col(gain[1:2, :])
    r0 = jnp.zeros((T, 1), F32)
    r1 = jnp.zeros((T, 1), F32)
    for c in range(4):
        cols = slice(c * 512, (c + 1) * 512)
        o = of[:, cols].astype(BF16)
        e0, e1 = dot(p0, o, 1, 0), dot(p1, o, 1, 0)
        ct = cot[:, cols].astype(F32)
        mixed[:, cols] = (g0 * e0 + g1 * e1).astype(BF16)
        r0 = r0 + jnp.sum(ct * e0, axis=1, keepdims=True)
        r1 = r1 + jnp.sum(ct * e1, axis=1, keepdims=True)
        tgrad[:, cols] = dot(both, df[:, cols].astype(BF16), 1, 0).astype(BF16)
    rgrad[0:1, :] = as_row(r0)
    rgrad[1:2, :] = as_row(r1)


def params(**kw):
    return pltpu.CompilerParams(vmem_limit_bytes=VMEM, **kw)


def cost(flops, nbytes):
    return pl.CostEstimate(flops=int(flops), bytes_accessed=int(nbytes), transcendentals=0)


VM = pl.BlockSpec(memory_space=pltpu.VMEM)


def local(tokens, cotangent, route_ids, route_weights, cold_gate, cold_up, cold_down, hot_gate, hot_up, hot_down):
    perm = jnp.asarray(packing(), BF16)
    perm_t = jnp.asarray(packing().T, BF16)
    ids_t, gain_t = route_ids.T, route_weights.T
    expert = lax.axis_index("expert")
    place = jnp.stack([lax.rem(expert, 2), lax.axis_index("dp")])

    right = [(i, (i + 1) % NDP) for i in range(NDP)]
    left = [(i, (i - 1) % NDP) for i in range(NDP)]
    own = jnp.concatenate([cold_gate[0], cold_up[0], cold_down[0]], axis=0)
    from_left = lax.ppermute(own, "dp", right)
    from_right = lax.ppermute(own, "dp", left)
    f_low = lax.ppermute(from_left[:HALF], "dp", right)
    f_up = lax.ppermute(from_right[HALF:], "dp", left)
    tokens, _ = lax.optimization_barrier((tokens, own))

    send, hot_rows = pl.pallas_call(
        dispatch_kernel,
        out_shape=(
            jax.ShapeDtypeStruct((OWN * CH * CAP, 256), BF16),
            jax.ShapeDtypeStruct((2 * HOT, D), BF16),
        ),
        in_specs=[VM] * 5,
        out_specs=(VM, VM),
        scratch_shapes=[pltpu.VMEM((SLOTS + HOT, D), F32), pltpu.VMEM((SLOTS + HOT, D), F32)],
        compiler_params=params(),
        cost_estimate=cost(4e9, 6e6),
    )(tokens, cotangent, ids_t, gain_t, perm)

    far = [(i, (i + 2) % NDP) for i in range(NDP)]
    hot_all = lax.all_gather(hot_rows, "dp", axis=0, tiled=True)
    arrived = lax.all_to_all(
        send.reshape(OWN, CH * CAP, 256), "expert", split_axis=0, concat_axis=0, tiled=True
    ).reshape(OWN * CH * CAP, 256)

    hot_all = lax.optimization_barrier((hot_all, from_left, from_right))[0]
    hot_other = lax.ppermute(hot_all, "expert", [(i, i ^ 1) for i in range(OWN)])
    hot_own, to_l, to_r, to_f, keep = pl.pallas_call(
        hot_kernel,
        out_shape=(
            jax.ShapeDtypeStruct((2 * HOT, D), BF16),
            jax.ShapeDtypeStruct((2 * HOT, D), BF16),
            jax.ShapeDtypeStruct((2 * HOT, D), BF16),
            jax.ShapeDtypeStruct((2 * HOT, D), BF16),
            jax.ShapeDtypeStruct((OWN // 2 * 48, 2 * Q), F32),
        ),
        in_specs=[pl.BlockSpec(memory_space=pltpu.SMEM)] + [VM] * 5,
        out_specs=(VM,) * 5,
        compiler_params=params(),
        cost_estimate=cost(3e10, 9e6),
    )(place, hot_all, hot_other, hot_gate, hot_up, hot_down)
    back_r = lax.ppermute(to_l, "dp", left)
    back_l = lax.ppermute(to_r, "dp", right)
    back_f = lax.ppermute(to_f, "dp", far)
    keep = lax.optimization_barrier((keep, f_low, f_up))[0]
    along_y = [[y * 16 + r for y in range(4)] for r in range(16)]
    along_z = [[y * 16 + z * 2 + c for z in range(8)] for y in range(4) for c in range(2)]
    hot_y = lax.psum_scatter(keep, "expert", scatter_dimension=0, axis_index_groups=along_y, tiled=True)
    half = jax.ShapeDtypeStruct((HALF, D), BF16)
    x, d, hid, gf_gate, gf_u, gf_v, gf_down = pl.pallas_call(
        far_kernel,
        out_shape=(
            jax.ShapeDtypeStruct((SLOTS, D), BF16),
            jax.ShapeDtypeStruct((SLOTS, D), BF16),
            jax.ShapeDtypeStruct((3, SLOTS, Q), BF16),
            jax.ShapeDtypeStruct((Q, D), BF16),
            jax.ShapeDtypeStruct((Q // 2, D), BF16),
            jax.ShapeDtypeStruct((Q // 2, D), BF16),
            jax.ShapeDtypeStruct((Q, D), BF16),
        ),
        in_specs=[VM] * 4,
        out_specs=(VM,) * 7,
        scratch_shapes=[pltpu.VMEM((SLOTS, D), F32), pltpu.VMEM((SLOTS, D), F32)],
        compiler_params=params(),
        cost_estimate=cost(4e9, 12e6),
    )(arrived, perm_t, f_low, f_up)
    came_gate = lax.ppermute(gf_gate, "dp", right)
    came_down = lax.ppermute(gf_down, "dp", left)
    came_u = lax.ppermute(gf_u, "dp", right)
    came_v = lax.ppermute(gf_v, "dp", left)
    hbm = pl.BlockSpec(memory_space=pl.ANY)
    back, mine = pl.pallas_call(
        near_kernel,
        out_shape=(
            jax.ShapeDtypeStruct((OWN * CH * CAP, 256), BF16),
            jax.ShapeDtypeStruct((3, SLOTS, 3 * Q), BF16),
        ),
        in_specs=[VM] * 4 + [hbm] * 5,
        out_specs=(VM, VM),
        scratch_shapes=[
            pltpu.VMEM((NDP * Q, D), BF16),
            pltpu.VMEM((NDP * Q, D), BF16),
            pltpu.VMEM((NDP * Q, D), BF16),
            pltpu.VMEM((SLOTS, D), F32),
            pltpu.VMEM((SLOTS, D), F32),
            pltpu.SemaphoreType.DMA((16,)),
        ],
        compiler_params=params(),
        cost_estimate=cost(1e6, 1e5),
    )(x, d, hid, perm, own, from_left, from_right, f_low, f_up)
    def shard_grads(shards, x, d):
        return pl.pallas_call(
            functools.partial(grad_kernel, shards),
            out_shape=(half,) * (2 * len(shards)),
            in_specs=[VM] * 3,
            out_specs=(VM,) * (2 * len(shards)),
            compiler_params=params(),
            cost_estimate=cost(1e6, 1e5),
        )(x, d, mine)

    gl_low, gl_up, gr_low, gr_up = shard_grads((1, 2), x, d)
    late_x = lax.optimization_barrier((x, came_u, came_v))[0]
    go_low, go_up = shard_grads((0,), late_x, d)
    gr_low, hot_y = lax.optimization_barrier((gr_low, hot_y))

    def plus(a, *b):
        return (a.astype(F32) + jnp.concatenate(b, axis=0).astype(F32)).astype(BF16)

    a_up = lax.ppermute(gr_up, "dp", right)
    b_low = lax.ppermute(gl_low, "dp", left)
    a_low = lax.ppermute(plus(gr_low, came_gate, came_u), "dp", right)
    b_up = lax.ppermute(plus(gl_up, came_v, came_down), "dp", left)
    back = lax.optimization_barrier((back, came_gate, came_down))[0]
    returned = lax.all_to_all(
        back.reshape(OWN, CH * CAP, 256), "expert", split_axis=0, concat_axis=0, tiled=True
    ).reshape(OWN * CH * CAP, 256)

    hot_z = lax.psum_scatter(hot_y, "expert", scatter_dimension=0, axis_index_groups=along_z, tiled=True)
    hot_low = hot_z[0:32].T
    hot_up_part = jnp.concatenate([hot_z[32:, :Q], hot_z[32:, Q:]], axis=0).T

    mixed, token_grad, route_grad = pl.pallas_call(
        combine_kernel,
        out_shape=(
            jax.ShapeDtypeStruct((T, D), BF16),
            jax.ShapeDtypeStruct((T, D), BF16),
            jax.ShapeDtypeStruct((2, T), F32),
        ),
        in_specs=[VM] * 9,
        out_specs=(VM, VM, VM),
        scratch_shapes=[pltpu.VMEM((SLOTS + HOT, D), F32), pltpu.VMEM((SLOTS + HOT, D), F32)],
        compiler_params=params(),
        cost_estimate=cost(4e9, 6e6),
    )(returned, hot_own, back_r, back_l, back_f, cotangent, ids_t, gain_t, perm_t)
    third = jax.ShapeDtypeStruct((1, Q, D), BF16)
    gate_grad, up_grad, down_grad = pl.pallas_call(
        finish_kernel,
        out_shape=(third,) * 3,
        grid=(4,),
        in_specs=[pl.BlockSpec((HALF, D // 4), lambda i: (0, i))] * 6,
        out_specs=(pl.BlockSpec((1, Q, D // 4), lambda i: (0, 0, i)),) * 3,
        compiler_params=params(),
        cost_estimate=cost(1e6, 10e6),
    )(go_low, go_up, a_low, a_up, b_low, b_up)
    return (
        mixed,
        token_grad,
        route_grad.T,
        gate_grad,
        up_grad,
        down_grad,
        hot_low[None, 0:Q],
        hot_low[None, Q:],
        hot_up_part[None],
    )


def solution(mesh):
    rows = P(("expert", "dp"), None)
    cold = P("expert", "dp", None)
    hot = P(None, "dp", None)
    split = P(None, "dp", "expert")
    return jax.shard_map(
        local,
        mesh=mesh,
        in_specs=(rows, rows, rows, rows, cold, cold, cold, hot, hot, hot),
        out_specs=(rows, rows, rows, cold, cold, cold, split, split, split),
        check_vma=False,
    )
```
